32 devices in a mesh: row: 4 (over z), col: 8 (over y, x, core).
Axes of the slice: x: 2, y: 2, z: 4, core: 2. Of those that a mesh axis runs over, the one named last changes fastest.
Arguments:
- factor_tiles: bfloat16 [3, 48, 64, 512], P(None, 'row', None, 'col'), may hold values from -0.3125 to 0.3125
- tile_row: int32 [3, 48, 8], P(None, 'row', 'col'), may hold values from 0 to 15
- tile_col: int32 [3, 48, 8], P(None, 'row', 'col'), may hold values from 0 to 7
- right_sides: float32 [4, 64, 64, 128], P(None, ('col', 'row')), may hold values from -6 to 6
- diag_inverse: float32 [4, 64, 4096], P(None, None, ('col', 'row')), as said below
Outputs:
- preconditioned: float32 [4, 64, 64, 128], P(None, ('col', 'row'))
The draws below stay inside these ranges and needn't reach their ends.
Inputs may be any that keep to these rules, and one draw needn't show every extreme that they name: `tile_row`: a block row within its row group. `tile_col`: a block column within its column group. `diag_inverse`: diagonal entries of every block between 0.5 and 2.
All inputs are finite; a program needn't handle non-finite values.
Results may differ from the reference program's by a relative error of at most 0.025.
Values may be sent and summed in bfloat16 or wider, within the bound.
No kernel may reach another device: no remote copies, remote signals or barrier semaphores. Data moves between devices by JAX's collectives and lax.ppermute only.
A program may use at most 64 MiB of HBM per device.

```python
import math
import jax
import jax.numpy as jnp
from jax import lax

BLOCK = 64
VECTORS = 128
ROWS_DEV = 2
TILE_SHARE = 6
LEVELS = 3
LEVEL_ROWS = 64
GROUP_ROWS = 8
LOCAL_ROWS = 16
TILES_DEV = 12
N_ROW = 4
N_COL = 8


def draw_diag_inverse(key, part):
    first_key, second_key = jax.random.split(key)
    shape = (LEVELS + 1, BLOCK, LEVEL_ROWS * BLOCK)
    noise = jax.random.normal(first_key, shape, jnp.float32)
    noise = noise * (0.4 / math.sqrt(BLOCK))
    diagonal = jnp.exp(jax.random.uniform(second_key, shape, jnp.float32, math.log(0.5), math.log(2.0)))
    column_pos = jnp.arange(shape[1], dtype=jnp.int32)[None, :, None]
    row_pos = jnp.arange(shape[2], dtype=jnp.int32)[None, None, :] % BLOCK
    return jnp.where(column_pos == row_pos, diagonal, noise)


def set_ends(entries, stream_key, least, high):
    place = [jax.random.randint(jax.random.fold_in(stream_key, axis), (), 0, length) for axis, length in enumerate(entries.shape)]
    longest = entries.shape.index(max(entries.shape))
    neighbour = place[:longest] + [(place[longest] + 1) % entries.shape[longest]] + place[longest + 1:]
    return entries.at[tuple(place)].set(least).at[tuple(neighbour)].set(high)


def block_scale(key, shape, cuts, smallest, largest):
    def one(axis_at, parts):
        steps = jax.random.uniform(jax.random.fold_in(jax.random.fold_in(key, 6), axis_at), (parts,), jnp.float32, smallest / len(cuts), largest / len(cuts))
        return jnp.repeat(jnp.exp(steps), shape[axis_at] // parts).reshape((-1,) + (1,) * (len(shape) - axis_at - 1))

    factor_of = one(*cuts[0])
    for cut in cuts[1:]:
        factor_of = factor_of * one(*cut)
    return factor_of


def normal_values(stream_key, shape, scale, most, cuts=(), kind=jnp.bfloat16):
    drawn = scale * jax.random.normal(stream_key, shape, jnp.float32)
    if cuts:
        drawn = drawn * block_scale(stream_key, shape, cuts, -0.22, 0.18)
    return jnp.clip(drawn, -most, most).astype(kind)


def setup_inputs(seed: int = 0) -> dict:
    seeds = jax.random.split(jax.random.key(seed), 6)
    return {
        "factor_tiles": normal_values(seeds[0], (LEVELS, N_ROW * TILES_DEV, BLOCK, N_COL * BLOCK), (TILE_SHARE * BLOCK) ** -0.5, 0.3125, ((1, 4), (3, 8))),
        "tile_row": set_ends(jax.random.randint(seeds[1], (LEVELS, N_ROW * TILES_DEV, N_COL), 0, LOCAL_ROWS), jax.random.fold_in(seeds[1], 1), 0, LOCAL_ROWS - 1).astype(jnp.int32),
        "tile_col": set_ends(jax.random.randint(seeds[2], (LEVELS, N_ROW * TILES_DEV, N_COL), 0, GROUP_ROWS), jax.random.fold_in(seeds[2], 1), 0, GROUP_ROWS - 1).astype(jnp.int32),
        "right_sides": normal_values(seeds[3], (LEVELS + 1, LEVEL_ROWS, BLOCK, VECTORS), 1.0, 6.0, ((1, 32),), jnp.float32),
        "diag_inverse": draw_diag_inverse(jax.random.fold_in(seeds[5], 71), 0),
    }


def apply_inverse(inverse, vector, transposed):
    matrix = inverse.reshape(inverse.shape[0], -1, inverse.shape[0])
    if transposed:
        return jnp.einsum("cir,irn->icn", matrix, vector, precision=lax.Precision.HIGHEST)
    return jnp.einsum("cir,icn->irn", matrix, vector, precision=lax.Precision.HIGHEST)


def rounded(value):
    return lax.optimization_barrier(value.astype(jnp.bfloat16)).astype(jnp.float32)


def reference(factor_tiles, tile_row, tile_col, right_sides, diag_inverse):
    tile_all = factor_tiles.reshape(LEVELS, N_ROW * TILES_DEV, BLOCK, N_COL, BLOCK).transpose(0, 1, 3, 2, 4)
    owner_group = (jnp.arange(N_ROW * TILES_DEV, dtype=jnp.int32) // TILES_DEV)[None, :, None]
    local_q = tile_row.astype(jnp.int32)
    global_rows = ((local_q // ROWS_DEV) * N_ROW + owner_group) * ROWS_DEV + local_q % ROWS_DEV
    global_cols = jnp.arange(N_COL, dtype=jnp.int32)[None, None, :] * GROUP_ROWS + tile_col.astype(jnp.int32)
    solved = [apply_inverse(diag_inverse[0], right_sides[0], False)]
    for section_no in range(1, LEVELS + 1):
        earlier = solved[-1].astype(jnp.bfloat16)

        def group_term(total, inputs, earlier=earlier):
            tile_block, row_block, col_block = inputs
            picked = earlier[col_block].astype(jnp.float32)
            product = jnp.einsum("tab,tbn->tan", tile_block.astype(jnp.float32), picked,
                                 precision=lax.Precision.HIGHEST)
            part = jax.ops.segment_sum(product, row_block, num_segments=LEVEL_ROWS)
            return total + rounded(part), None

        inputs = (tile_all[section_no - 1].transpose(1, 0, 2, 3),
                  global_rows[section_no - 1].T, global_cols[section_no - 1].T)
        initial = jnp.zeros((LEVEL_ROWS, BLOCK, VECTORS), jnp.float32)
        coupled, unused = lax.scan(group_term, initial, inputs)
        solved.append(apply_inverse(diag_inverse[section_no], right_sides[section_no] - coupled, False))
    result = [None] * (LEVELS + 1)
    result[LEVELS] = apply_inverse(diag_inverse[LEVELS], solved[LEVELS], True)
    for section_no in range(LEVELS - 1, -1, -1):
        upper = result[section_no + 1].astype(jnp.bfloat16)

        def row_term(total, inputs, upper=upper):
            tile_block, row_block, col_block = inputs
            picked = upper[row_block].astype(jnp.float32)
            spread = jnp.einsum("tab,tan->tbn", tile_block.astype(jnp.float32), picked,
                                precision=lax.Precision.HIGHEST)
            part = jax.ops.segment_sum(spread, col_block, num_segments=LEVEL_ROWS)
            return total + rounded(part), None

        inputs = (tile_all[section_no].reshape(N_ROW, TILES_DEV * N_COL, BLOCK, BLOCK),
                  global_rows[section_no].reshape(N_ROW, TILES_DEV * N_COL),
                  global_cols[section_no].reshape(N_ROW, TILES_DEV * N_COL))
        initial = jnp.zeros((LEVEL_ROWS, BLOCK, VECTORS), jnp.float32)
        back, unused = lax.scan(row_term, initial, inputs)
        result[section_no] = apply_inverse(diag_inverse[section_no], solved[section_no] - back, True)
    return jnp.stack(result)
```

```python
import functools

import jax
import jax.numpy as jnp
from jax import lax
from jax.experimental import pallas as pl
from jax.experimental.pallas import tpu as pltpu
from jax.sharding import PartitionSpec as P

BF16 = jnp.bfloat16
F32 = jnp.float32
NT = (((1,), (1,)), ((), ()))
VMEM_BYTES = 24 << 20
SLICE_ROWS = 16


class Plan:
    def __init__(self, n_row, n_col, factor_tiles, right_sides):
        self.levels, self.tiles, self.block, _ = factor_tiles.shape
        self.rows_dev = right_sides.shape[1]
        self.vectors = right_sides.shape[3]
        self.n_row, self.n_col = n_row, n_col
        split = 1
        while n_col % (split * 2) == 0 and self.vectors // (n_row * split * 2) >= SLICE_ROWS:
            split *= 2
        self.split = split
        self.groups = n_col // split
        self.sources = n_row * split
        self.slice = self.vectors // self.sources
        self.lanes = self.rows_dev * self.block
        self.owned = self.sources * self.rows_dev
        self.blocks = self.groups * self.owned
        self.tile_rows = self.tiles // 2 * self.block
        self.levels_in = [[0]] + [[s] for s in range(1, self.levels - 1)] + [[self.levels - 1, self.levels]]
        self.index_at = self.tile_rows
        self.inverse_at = self.index_at + 16

    def vector_parts(self, coupling):
        return 1 if coupling == 0 else 2 * len(self.levels_in[coupling])

    def vectors_at(self, coupling):
        inverses = 0 if coupling == 0 else len(self.levels_in[coupling])
        return self.inverse_at + inverses * self.block

    def payload_rows(self, coupling):
        return self.vectors_at(coupling) + self.split * self.vector_parts(coupling) * self.slice

    def pieces(self):
        return [(mz, my) for my in range(self.split) for mz in range(self.n_row)]


def call(body, outs, specs, scratch, args):
    return pl.pallas_call(
        body,
        out_shape=outs,
        in_specs=specs,
        out_specs=[pl.BlockSpec(memory_space=pltpu.VMEM)] * len(outs),
        scratch_shapes=scratch,
        compiler_params=pltpu.CompilerParams(vmem_limit_bytes=VMEM_BYTES),
    )(*args)


def vmem(count):
    return [pl.BlockSpec(memory_space=pltpu.VMEM)] * count


def smem(count):
    return [pl.BlockSpec(memory_space=pltpu.SMEM)] * count


def low_lanes(shape, half):
    return lax.broadcasted_iota(jnp.int32, shape, len(shape) - 1) < half


def split_rows(value):
    high = value.astype(BF16)
    return jnp.concatenate([high, (value - high.astype(F32)).astype(BF16)], axis=0)


def apply_pair(inverse, value, half):
    n = value.shape[0]
    both = jnp.concatenate([value, pltpu.roll(value, half, 1)], axis=0)[:, :half]
    out = jnp.dot(split_rows(both), inverse, preferred_element_type=F32)
    out = out[: 2 * n] + out[2 * n :]
    return jnp.where(low_lanes((n, 2 * half), half), out[:n], out[n:])


def apply_pair_transposed(inverse, value, half):
    n = value.shape[0]
    low = low_lanes(value.shape, half)
    both = jnp.concatenate([jnp.where(low, value, 0.0), jnp.where(low, 0.0, value)], axis=0)
    out = lax.dot_general(split_rows(both), inverse, NT, preferred_element_type=F32)
    out = out[: 2 * n] + out[2 * n :]
    return jnp.concatenate([out[:n], out[n:]], axis=1)


def pack_tiles(plan, coupling, tiles, rows, cols, payloads):
    lane = lax.broadcasted_iota(jnp.int32, (16, 128), 1)
    index = jnp.zeros((16, 128), F32)
    for t in range(plan.tiles):
        index = jnp.where(lane == t, rows[coupling, t, 0].astype(F32), index)
        index = jnp.where(lane == t + 64, cols[coupling, t, 0].astype(F32), index)
    index = index.astype(BF16)
    for k in range(plan.tiles // 2):
        pair = jnp.concatenate([tiles[coupling, 2 * k], tiles[coupling, 2 * k + 1]], axis=1)
        for payload in payloads:
            payload[k * plan.block : (k + 1) * plan.block, :] = pair
    for payload in payloads:
        payload[plan.index_at : plan.index_at + 16, :] = index


def put_slices(plan, coupling, part, place, scratch, payloads):
    width = plan.slice
    for mz, payload in enumerate(payloads):
        for my in range(plan.split):
            number = (place[0] ^ mz) * plan.split + (place[1] ^ my)
            at = plan.vectors_at(coupling) + (my * plan.vector_parts(coupling) + part) * width
            payload[at : at + width, :] = scratch[number]


def first_kernel(plan, place, rows, cols, tiles, sides, inverse, *rest):
    payloads, x0, scratch = rest[: plan.n_row], rest[plan.n_row], rest[plan.n_row + 1]
    half = plan.block
    parts = []
    for b in range(plan.rows_dev):
        matrix = inverse[0, :, b * half : (b + 1) * half]
        parts.append(lax.dot_general(matrix, sides[0, b], (((0,), (0,)), ((), ())),
                                     precision=lax.Precision.HIGHEST, preferred_element_type=F32))
    solved = jnp.concatenate(parts, axis=0)
    x0[...] = solved
    scratch[...] = solved.T.astype(BF16).reshape(scratch.shape)
    pack_tiles(plan, 0, tiles, rows, cols, payloads)
    put_slices(plan, 0, 0, place, scratch, payloads)


def second_kernel(plan, place, rows, cols, tiles, sides, inverse, *rest):
    scratch = rest[-1]
    half = plan.block
    for coupling in range(1, plan.levels):
        payloads = rest[(coupling - 1) * plan.n_row : coupling * plan.n_row]
        pack_tiles(plan, coupling, tiles, rows, cols, payloads)
        for at, level in enumerate(plan.levels_in[coupling]):
            start = plan.inverse_at + at * half
            matrix = inverse[level].astype(BF16)
            for payload in payloads:
                payload[start : start + half, :] = matrix
            both = jnp.concatenate([sides[level, b] for b in range(plan.rows_dev)], axis=0).T
            high = both.astype(BF16)
            low = (both - high.astype(F32)).astype(BF16)
            for part, value in enumerate((high, low)):
                scratch[at, part] = value.reshape(scratch.shape[2:])
                put_slices(plan, coupling, 2 * at + part, place, scratch.at[at, part], payloads)


def vector_slice(plan, coupling, piece, my, part):
    at = plan.vectors_at(coupling) + (my * plan.vector_parts(coupling) + part) * plan.slice
    return piece[at : at + plan.slice, :]


def source(plan, place, mz, my):
    return (place[1] ^ my) * plan.n_row + (place[0] ^ mz)


def decode(plan, place, pieces, index):
    lane = lax.broadcasted_iota(jnp.int32, (1, 128), 1)
    for p, (mz, my) in enumerate(plan.pieces()):
        raw = pieces[p][plan.index_at : plan.index_at + 16, :].astype(F32).astype(jnp.int32)[0:1]
        owner = raw // plan.rows_dev
        group, part = owner % plan.groups, owner // plan.groups
        row = group * plan.owned + (part * plan.n_row + (place[0] ^ mz)) * plan.rows_dev + raw % plan.rows_dev
        col = (place[1] ^ my) * (plan.n_row * plan.rows_dev) + raw
        index[p : p + 1, :] = jnp.where(lane < 64, row, col)


def store_halves(left, right, at, value, half):
    low = low_lanes(value.shape, half)
    other = pltpu.roll(value, half, 1)
    left[2 * at] = jnp.where(low, value, 0.0).astype(BF16)
    right[2 * at] = jnp.where(low, 0.0, other).astype(BF16)
    left[2 * at + 1] = jnp.where(low, other, 0.0).astype(BF16)
    right[2 * at + 1] = jnp.where(low, 0.0, value).astype(BF16)


def forward_kernel(plan, coupling, *refs):
    refs = list(refs)
    place = refs.pop(0)
    take = lambda count: [refs.pop(0) for _ in range(count)]
    pieces = take(plan.sources)
    sums = take(plan.groups) if coupling else None
    out = take(plan.groups)
    index_out = refs.pop(0)
    solved = refs.pop(0) if coupling else None
    left, right, total, index, sem = refs
    half, width = plan.block, plan.slice
    decode(plan, place, pieces, index_out)
    copy = pltpu.make_async_copy(index_out, index, sem)
    copy.start()
    for p, (mz, my) in enumerate(plan.pieces()):
        at = source(plan, place, mz, my)
        if coupling == 0:
            value = vector_slice(plan, 0, pieces[p], my, 0).astype(F32)
        else:
            value = level_solve(plan, coupling, 0, pieces[p], my, sums, at)
            solved[at] = value
        store_halves(left, right, at, value, half)
    total[...] = jnp.zeros_like(total)
    copy.wait()
    for p in range(plan.sources):
        for k in range(plan.tiles // 2):
            pair = pieces[p][k * half : (k + 1) * half, :]
            vectors = jnp.concatenate([left[index[p, 2 * k + 64]], right[index[p, 2 * k + 65]]], axis=0)
            product = lax.dot_general(vectors, pair, NT, preferred_element_type=F32)
            total[index[p, 2 * k]] += product[:width]
            total[index[p, 2 * k + 1]] += product[width:]
    for m in range(plan.groups):
        base = (place[2] ^ m) * plan.owned
        for u in range(plan.sources):
            value = jnp.concatenate([total[base + 2 * u], total[base + 2 * u + 1]], axis=1)
            out[m][u] = value.astype(out[m].dtype)


def level_solve(plan, coupling, at_level, piece, my, sums, at):
    coupled = sums[0][at]
    for received in sums[1:]:
        coupled = coupled + received[at].astype(F32)
    value = vector_slice(plan, coupling, piece, my, 2 * at_level).astype(F32)
    value = value + vector_slice(plan, coupling, piece, my, 2 * at_level + 1).astype(F32)
    start = plan.inverse_at + at_level * plan.block
    return apply_pair(piece[start : start + plan.block, :], value - coupled, plan.block)


def top_kernel(plan, place, *refs):
    pieces, sums, out = refs[: plan.sources], refs[plan.sources : -1], refs[-1]
    start = plan.inverse_at + plan.block
    for p, (mz, my) in enumerate(plan.pieces()):
        at = source(plan, place, mz, my)
        value = level_solve(plan, plan.levels - 1, 1, pieces[p], my, sums, at)
        out[at] = apply_pair_transposed(pieces[p][start : start + plan.block, :], value, plan.block).astype(BF16)


def backward_kernel(plan, coupling, *refs):
    refs = list(refs)
    place, index = refs.pop(0), refs.pop(0)
    take = lambda count: [refs.pop(0) for _ in range(count)]
    pieces = take(plan.sources)
    upper = take(plan.groups)
    solved = refs.pop(0) if coupling else None
    earlier = None if coupling else take(plan.levels)
    out = [refs.pop(0)] if coupling else take(plan.sources)
    rows, left, right = refs
    half, width = plan.block, plan.slice
    for m in range(plan.groups):
        base = (place[2] ^ m) * plan.owned
        for u in range(plan.sources):
            value = upper[m][u]
            rows[base + 2 * u] = value[:, :half]
            rows[base + 2 * u + 1] = value[:, half:]
    left[...] = jnp.zeros_like(left)
    right[...] = jnp.zeros_like(right)
    for p in range(plan.sources):
        for k in range(plan.tiles // 2):
            pair = pieces[p][k * half : (k + 1) * half, :]
            vectors = jnp.concatenate([rows[index[p, 2 * k]], rows[index[p, 2 * k + 1]]], axis=0)
            product = jnp.dot(vectors, pair, preferred_element_type=F32)
            left[index[p, 2 * k + 64]] += product[:width]
            right[index[p, 2 * k + 65]] += product[width:]
    low = low_lanes((width, plan.lanes), half)
    for p, (mz, my) in enumerate(plan.pieces()):
        at = source(plan, place, mz, my)
        first = left[2 * at] + pltpu.roll(right[2 * at], half, 1)
        other = right[2 * at + 1] + pltpu.roll(left[2 * at + 1], half, 1)
        back = jnp.where(low, first, other)
        if coupling:
            start = plan.inverse_at
            value = apply_pair_transposed(pieces[p][start : start + half, :], solved[at] - back, half)
            out[0][at] = value.astype(BF16)
        else:
            for n, level in enumerate(earlier):
                out[p][n * width : (n + 1) * width, :] = level[at]
            out[p][plan.levels * width :, :] = back.astype(BF16)


def last_kernel(plan, place, inverse, x0, *refs):
    pieces, out, scratch = refs[: plan.sources], refs[plan.sources], refs[plan.sources + 1]
    half, width = plan.block, plan.slice
    for p, (mz, my) in enumerate(plan.pieces()):
        number = (place[0] ^ mz) * plan.split + (place[1] ^ my)
        for n in range(plan.levels + 1):
            scratch[n, number] = pieces[p][n * width : (n + 1) * width, :]
    for n in range(plan.levels + 1):
        value = scratch[n].astype(F32).reshape(plan.vectors, plan.lanes).T
        if n == plan.levels:
            value = x0[...] - value
        for b in range(plan.rows_dev):
            part = value[b * half : (b + 1) * half, :]
            if n == plan.levels:
                part = jnp.dot(inverse[0, :, b * half : (b + 1) * half], part,
                               precision=lax.Precision.HIGHEST, preferred_element_type=F32)
            out[plan.levels - n if n < plan.levels else 0, b] = part


def on_device(n_row, n_col, factor_tiles, tile_row, tile_col, right_sides, diag_inverse):
    plan = Plan(n_row, n_col, factor_tiles, right_sides)
    levels, groups, sources = plan.levels, plan.groups, plan.sources
    shape = jax.ShapeDtypeStruct
    r, c = lax.axis_index("row"), lax.axis_index("col")
    place = jnp.stack([r, c // groups, c % groups]).astype(jnp.int32)

    def move(value, mz, my, mg):
        if mz == 0:
            pairs = [(i, i ^ (my * groups + mg)) for i in range(n_col)]
            return lax.ppermute(value, "col", pairs)
        if my == 0 and mg == 0:
            return lax.ppermute(value, "row", [(i, i ^ mz) for i in range(n_row)])
        pairs = [(i, i ^ (mz * n_col + my * groups + mg)) for i in range(n_row * n_col)]
        return lax.ppermute(value, ("row", "col"), pairs)

    def gather(payloads):
        near = [payloads[0]] + [move(payloads[mz], mz, 0, 0) for mz in range(1, n_row)]
        return [near[mz] if my == 0 else move(near[mz], 0, my, 0) for mz, my in plan.pieces()]

    piece_shape = (sources, plan.slice, plan.lanes)
    common = (place, tile_row, tile_col, factor_tiles, right_sides, diag_inverse)
    specs = smem(3) + vmem(3)
    made = call(
        functools.partial(first_kernel, plan),
        [shape((plan.payload_rows(0), plan.lanes), BF16)] * n_row + [shape((plan.lanes, plan.vectors), F32)],
        specs,
        [pltpu.VMEM(piece_shape, BF16)],
        common,
    )
    x0 = made[n_row]
    payloads = [made[:n_row]]
    made = call(
        functools.partial(second_kernel, plan),
        [shape((plan.payload_rows(s), plan.lanes), BF16) for s in range(1, levels) for _ in range(n_row)],
        specs,
        [pltpu.VMEM((2, 2) + piece_shape, BF16)],
        common,
    )
    payloads += [made[s * n_row : (s + 1) * n_row] for s in range(levels - 1)]
    pieces = [gather(payload) for payload in payloads]

    piece = shape(piece_shape, BF16)
    index_shape = (max(8, sources), 128)
    scratch = [
        pltpu.VMEM((plan.owned, plan.slice, plan.lanes), BF16),
        pltpu.VMEM((plan.owned, plan.slice, plan.lanes), BF16),
        pltpu.VMEM((plan.blocks, plan.slice, plan.block), F32),
        pltpu.SMEM(index_shape, jnp.int32),
        pltpu.SemaphoreType.DMA(()),
    ]
    index, solved, sums = [], [None], None
    for s in range(levels):
        args = [place] + pieces[s] + (sums if s else [])
        outs = [shape(piece_shape, F32)] + [piece] * (groups - 1) + [shape(index_shape, jnp.int32)]
        outs += [shape(piece_shape, F32)] if s else []
        body = functools.partial(forward_kernel, plan, s)
        made = call(body, outs, smem(1) + vmem(len(args) - 1), scratch, args)
        sums = [made[0]] + [move(made[m], 0, 0, m) for m in range(1, groups)]
        index.append(made[groups])
        if s:
            solved.append(made[groups + 1])
    args = [place] + pieces[levels - 1] + sums
    current = call(functools.partial(top_kernel, plan), [piece], smem(1) + vmem(len(args) - 1), [], args)[0]
    results = [current]
    scratch = [
        pltpu.VMEM((plan.blocks, plan.slice, plan.block), BF16),
        pltpu.VMEM((plan.owned, plan.slice, plan.lanes), F32),
        pltpu.VMEM((plan.owned, plan.slice, plan.lanes), F32),
    ]
    for s in range(levels - 1, -1, -1):
        upper = [current] + [move(current, 0, 0, m) for m in range(1, groups)]
        args = [place, index[s]] + pieces[s] + upper + ([solved[s]] if s else results)
        outs = [piece] if s else [shape(((levels + 1) * plan.slice, plan.lanes), BF16)] * sources
        made = call(functools.partial(backward_kernel, plan, s), outs, smem(2) + vmem(len(args) - 2), scratch, args)
        if s:
            current = made[0]
            results.append(current)
    final = [made[p] if (mz, my) == (0, 0) else move(made[p], mz, my, 0) for p, (mz, my) in enumerate(plan.pieces())]
    args = [place, diag_inverse, x0] + final
    return call(
        functools.partial(last_kernel, plan),
        [shape(right_sides.shape, F32)],
        smem(1) + vmem(len(args) - 1),
        [pltpu.VMEM((levels + 1,) + piece_shape, BF16)],
        args,
    )[0]


def solution(mesh):
    return jax.shard_map(
        functools.partial(on_device, mesh.shape["row"], mesh.shape["col"]),
        mesh=mesh,
        in_specs=(
            P(None, "row", None, "col"),
            P(None, "row", "col"),
            P(None, "row", "col"),
            P(None, ("col", "row"), None, None),
            P(None, None, ("col", "row")),
        ),
        out_specs=P(None, ("col", "row"), None, None),
        check_vma=False,
    )
```

```python
import functools

import jax
import jax.numpy as jnp
from jax import lax
from jax.experimental import pallas as pl
from jax.experimental.pallas import tpu as pltpu
from jax.sharding import PartitionSpec as P

BF16 = jnp.bfloat16
F32 = jnp.float32
NT = (((1,), (1,)), ((), ()))
TN = (((0,), (0,)), ((), ()))
SLICE_ROWS = 16


class Plan:
    def __init__(self, n_row, n_col, factor_tiles, right_sides):
        self.levels, self.tiles, self.block, _ = factor_tiles.shape
        self.rows_dev = right_sides.shape[1]
        self.vectors = right_sides.shape[3]
        self.n_row, self.n_col, self.chips = n_row, n_col, n_col // 2
        self.real = self.vectors // n_col
        self.slice = max(SLICE_ROWS, self.real)
        self.padded = self.slice * n_col
        self.lanes = self.rows_dev * self.block
        self.own = n_col * self.rows_dev
        self.blocks = n_row * self.own
        self.tile_rows = self.tiles // 2 * self.block
        self.index_at = self.tile_rows
        self.inverse_at = self.index_at + 16
        self.vmem_bytes = (24 if n_col <= 8 else 48) << 20

    def inverse_rows(self, level):
        return pl.ds(self.inverse_at + (level - 1) * self.block, self.block)

    def sides_at(self, level, core=0):
        start = self.inverse_at + self.levels * self.block
        return start + ((level - 1) * 2 + core) * self.slice

    def first_rows(self):
        return self.sides_at(self.levels + 1)

    def sources(self):
        return [2 * chip + core for core in range(2) for chip in range(self.chips)]


def call(plan, body, outs, args, scratch=(), scalars=1, raw=()):
    specs = [pl.BlockSpec(memory_space=pltpu.SMEM)] * scalars
    specs += [pl.BlockSpec(memory_space=pltpu.HBM if n in raw else pltpu.VMEM) for n in range(scalars, len(args))]
    return pl.pallas_call(
        functools.partial(body, plan),
        out_shape=outs,
        in_specs=specs,
        out_specs=[pl.BlockSpec(memory_space=pltpu.VMEM)] * len(outs),
        scratch_shapes=list(scratch),
        compiler_params=pltpu.CompilerParams(vmem_limit_bytes=plan.vmem_bytes),
    )(*args)


def take(refs, count):
    return [refs.pop(0) for _ in range(count)]


def low_lanes(shape, half):
    return lax.broadcasted_iota(jnp.int32, shape, len(shape) - 1) < half


def split_rows(value):
    high = value.astype(BF16)
    return jnp.concatenate([high, (value - high.astype(F32)).astype(BF16)], axis=0)


def apply_pair(inverse, value, half):
    n = value.shape[0]
    both = jnp.concatenate([value, pltpu.roll(value, half, 1)], axis=0)[:, :half]
    out = jnp.dot(split_rows(both), inverse, preferred_element_type=F32)
    out = out[: 2 * n] + out[2 * n :]
    return jnp.where(low_lanes((n, 2 * half), half), out[:n], out[n:])


def apply_pair_transposed(inverse, value, half):
    n = value.shape[0]
    low = low_lanes(value.shape, half)
    both = jnp.concatenate([jnp.where(low, value, 0.0), jnp.where(low, 0.0, value)], axis=0)
    out = lax.dot_general(split_rows(both), inverse, NT, preferred_element_type=F32)
    out = out[: 2 * n] + out[2 * n :]
    return jnp.concatenate([out[:n], out[n:]], axis=1)


def pad_slices(plan, value, out):
    if plan.real == plan.slice:
        out[...] = value.astype(out.dtype)
        return
    out[...] = jnp.zeros_like(out)
    for c in range(plan.n_col):
        out[c * plan.slice : c * plan.slice + plan.real, :] = value[c * plan.real : (c + 1) * plan.real].astype(out.dtype)


def drop_padding(plan, value):
    if plan.real == plan.slice:
        return value
    return jnp.concatenate([value[c * plan.slice : c * plan.slice + plan.real] for c in range(plan.n_col)], axis=0)


def store_halves(left, right, at, value, half):
    low = low_lanes(value.shape, half)
    other = pltpu.roll(value, half, 1)
    left[2 * at] = jnp.where(low, value, 0.0).astype(BF16)
    right[2 * at] = jnp.where(low, 0.0, other).astype(BF16)
    left[2 * at + 1] = jnp.where(low, other, 0.0).astype(BF16)
    right[2 * at + 1] = jnp.where(low, 0.0, value).astype(BF16)


def join_halves(left, right, at, half):
    first = left[2 * at] + pltpu.roll(right[2 * at], half, 1)
    second = right[2 * at + 1] + pltpu.roll(left[2 * at + 1], half, 1)
    return jnp.where(low_lanes(first.shape, half), first, second)


def first_kernel(plan, sides, inverse, solved, message, sides_here, inverse_here, sems):
    copies = [
        pltpu.make_async_copy(sides.at[0], sides_here, sems.at[0]),
        pltpu.make_async_copy(inverse.at[0], inverse_here, sems.at[1]),
    ]
    for copy in copies:
        copy.start()
    for copy in copies:
        copy.wait()
    parts = [
        lax.dot_general(sides_here[b], inverse_here[:, b * plan.block : (b + 1) * plan.block], TN,
                        precision=lax.Precision.HIGHEST, preferred_element_type=F32)
        for b in range(plan.rows_dev)
    ]
    pad_slices(plan, jnp.concatenate(parts, axis=1), solved)
    message[...] = solved[...].astype(BF16)


def pack_kernel(plan, place, rows, cols, *refs):
    refs = list(refs)
    tiles, sides, inverse = take(refs, 3)
    first = refs.pop(0)
    payloads = [None, take(refs, plan.chips)] + [[ref.at[0]] for ref in take(refs, plan.levels - 2)]
    tiles_here, sides_here, inverse_here, slices, sems = refs
    copies = [
        pltpu.make_async_copy(tiles, tiles_here, sems.at[0]),
        pltpu.make_async_copy(sides, sides_here, sems.at[1]),
        pltpu.make_async_copy(inverse, inverse_here, sems.at[2]),
    ]
    for copy in copies:
        copy.start()
    for copy in copies:
        copy.wait()
    half, width = plan.block, plan.slice
    lane = lax.broadcasted_iota(jnp.int32, (16, 128), 1)
    for coupling in range(plan.levels):
        targets = [first] if coupling == 0 else payloads[coupling]
        for k in range(plan.tiles // 2):
            pair = jnp.concatenate([tiles_here[coupling, 2 * k], tiles_here[coupling, 2 * k + 1]], axis=1)
            for target in targets:
                target[k * half : (k + 1) * half, :] = pair
        if coupling == 0:
            continue
        index = jnp.zeros((16, 128), F32)
        for t in range(plan.tiles):
            index = jnp.where(lane == t, rows[coupling, t, 0].astype(F32), index)
            index = jnp.where(lane == t + 64, cols[coupling, t, 0].astype(F32), index)
        for target in targets:
            target[plan.index_at : plan.index_at + 16, :] = index.astype(BF16)
        if coupling > 1:
            continue
        for level in range(1, plan.levels + 1):
            matrix = inverse_here[level].astype(BF16)
            both = jnp.concatenate([sides_here[level, b] for b in range(plan.rows_dev)], axis=0).T
            pad_slices(plan, both, slices)
            for chip, target in enumerate(targets):
                target[plan.inverse_rows(level), :] = matrix
                base = (place[1] ^ (2 * chip)) // 2 * 2
                for core in range(2):
                    here = pl.ds(pl.multiple_of((base + core) * width, 16), width)
                    start = plan.sides_at(level, core)
                    target[start : start + width, :] = slices[here, :]


def near_forward_kernel(plan, place, rows, cols, pairs, *refs):
    refs = list(refs)
    received = take(refs, plan.n_row)
    keep, send, left, right, total = refs
    half, width = plan.block, plan.slice
    for m in range(plan.n_row):
        store_halves(left, right, place[0] ^ m, received[m][...].astype(F32), half)
    total[...] = jnp.zeros_like(total)
    for k in range(plan.tiles // 2):
        pair = pairs[k * half : (k + 1) * half, :]
        vectors = jnp.concatenate([left[cols[0, 2 * k, 0]], right[cols[0, 2 * k + 1, 0]]], axis=0)
        product = lax.dot_general(vectors, pair, NT, preferred_element_type=F32)
        total[rows[0, 2 * k, 0]] += product[: plan.padded]
        total[rows[0, 2 * k + 1, 0]] += product[plan.padded :]
    for chip in range(plan.chips):
        for core, out in enumerate((keep, send)):
            number = place[1] ^ (2 * chip + core)
            here = pl.ds(pl.multiple_of(number * width, 16), width)
            for u in range(plan.n_col):
                value = jnp.concatenate([total[2 * u, here, :], total[2 * u + 1, here, :]], axis=1)
                out[chip, u] = value.astype(out.dtype)


def add_kernel(plan, keep, received, *out):
    for chip in range(plan.chips):
        out[chip][...] = (keep[chip] + received[chip].astype(F32)).astype(out[chip].dtype)


def near_backward_kernel(plan, place, rows, cols, pairs, *refs):
    refs = list(refs)
    received = take(refs, plan.n_col)
    out = take(refs, plan.n_row)
    upper, left, right = refs
    half, width = plan.block, plan.slice
    for piece, offset in zip(received, plan.sources()):
        here = pl.ds(pl.multiple_of((place[1] ^ offset) * width, 16), width)
        for u in range(plan.n_col):
            value = piece[u]
            upper[2 * u, here, :] = value[:, :half]
            upper[2 * u + 1, here, :] = value[:, half:]
    left[...] = jnp.zeros_like(left)
    right[...] = jnp.zeros_like(right)
    for k in range(plan.tiles // 2):
        pair = pairs[k * half : (k + 1) * half, :]
        vectors = jnp.concatenate([upper[rows[0, 2 * k, 0]], upper[rows[0, 2 * k + 1, 0]]], axis=0)
        product = jnp.dot(vectors, pair, preferred_element_type=F32)
        left[cols[0, 2 * k, 0]] += product[: plan.padded]
        right[cols[0, 2 * k + 1, 0]] += product[plan.padded :]
    for m in range(plan.n_row):
        out[m][...] = join_halves(left, right, place[0] ^ m, half).astype(out[m].dtype)


def last_kernel(plan, place, *refs):
    refs = list(refs)
    inverse, solved = take(refs, 2)
    shares = take(refs, plan.n_row)
    pieces = take(refs, plan.n_col)
    out, all_slices = refs
    half, width = plan.block, plan.slice
    core = place[1] & 1
    for piece, offset in zip(pieces, plan.sources()):
        here = pl.ds(pl.multiple_of((place[1] ^ offset) * width, 16), width)
        all_slices[0, here, :] = piece[place[1]]
        for n in range(1, plan.levels):
            all_slices[n, here, :] = piece[plan.n_col + core * (plan.levels - 1) + n - 1]
    for n in range(plan.levels):
        value = drop_padding(plan, all_slices[n].astype(F32)).T
        for b in range(plan.rows_dev):
            out[n + 1, b] = value[b * half : (b + 1) * half, :]
    back = shares[0][...]
    for share in shares[1:]:
        back = back + share[...].astype(F32)
    value = drop_padding(plan, solved[...] - back)
    for b in range(plan.rows_dev):
        cut = slice(b * half, (b + 1) * half)
        out[0, b] = lax.dot_general(inverse[0, :, cut], value[:, cut], NT,
                                    precision=lax.Precision.HIGHEST, preferred_element_type=F32)


def level_forward(plan, place, level, pieces, coupled, write):
    for piece, offset in zip(pieces, plan.sources()):
        u = place[1] ^ offset
        start = plan.sides_at(level) + (place[1] & 1) * plan.slice
        side = piece[pl.ds(pl.multiple_of(start, 16), plan.slice), :].astype(F32)
        write(piece, u, apply_pair(piece[plan.inverse_rows(level), :], side - coupled(u), plan.block))


def level_backward(plan, place, level, pieces, value, write):
    for piece, offset in zip(pieces, plan.sources()):
        u = place[1] ^ offset
        write(u, apply_pair_transposed(piece[plan.inverse_rows(level), :], value(u), plan.block))


def join_kernel(plan, first, second, out):
    count = first.shape[0]
    out[:count] = first[...]
    out[count:] = second[...]


def views(plan, refs):
    if len(refs) == plan.n_col:
        return refs
    return [ref.at[chip] for ref in refs for chip in range(plan.chips)]


def add_up(refs):
    def total(u):
        value = refs[0][u]
        for ref in refs[1:]:
            value = value + ref[u].astype(F32)
        return value

    return total


def enter_kernel(plan, place, *refs):
    refs = list(refs)
    pieces, sums = take(refs, plan.n_col), take(refs, plan.chips)
    solved, message = refs

    def write(piece, u, value):
        solved[u] = value
        message[u] = value.astype(BF16)

    level_forward(plan, place, 1, pieces, add_up(sums), write)


def decode(plan, place, pieces, index):
    lane = lax.broadcasted_iota(jnp.int32, (1, 128), 1)
    for p, offset in enumerate(plan.sources()):
        raw = pieces[p][plan.index_at : plan.index_at + 16, :].astype(F32).astype(jnp.int32)[0:1]
        owner = raw // plan.rows_dev * plan.n_col + (place[1] ^ offset)
        col = owner * plan.rows_dev + raw % plan.rows_dev
        index[p : p + 1, :] = jnp.where(lane < 64, raw, col)


def multiply_forward(plan, place, pieces, received, index, left, right, total, ready):
    half, width = plan.block, plan.slice
    for m in range(plan.n_row):
        for u in range(plan.n_col):
            store_halves(left, right, (place[0] ^ m) * plan.n_col + u, received[m][u].astype(F32), half)
    total[...] = jnp.zeros_like(total)
    ready()
    for p in range(plan.n_col):
        for k in range(plan.tiles // 2):
            pair = pieces[p][k * half : (k + 1) * half, :]
            vectors = jnp.concatenate([left[index[p, 2 * k + 64]], right[index[p, 2 * k + 65]]], axis=0)
            product = lax.dot_general(vectors, pair, NT, preferred_element_type=F32)
            total[index[p, 2 * k]] += product[:width]
            total[index[p, 2 * k + 1]] += product[width:]


def multiply_backward(plan, place, pieces, index, upper, left, right, out):
    half, width = plan.block, plan.slice
    for p in range(plan.n_col):
        for k in range(plan.tiles // 2):
            pair = pieces[p][k * half : (k + 1) * half, :]
            vectors = jnp.concatenate([upper[index[p, 2 * k]], upper[index[p, 2 * k + 1]]], axis=0)
            product = jnp.dot(vectors, pair, preferred_element_type=F32)
            left[index[p, 2 * k + 64]] += product[:width]
            right[index[p, 2 * k + 65]] += product[width:]
    for m in range(plan.n_row):
        for u in range(plan.n_col):
            at = (place[0] ^ m) * plan.n_col + u
            out[m][u] = join_halves(left, right, at, half).astype(out[m].dtype)


def put_upper(plan, upper, u, value):
    upper[2 * u] = value[:, : plan.block].astype(BF16)
    upper[2 * u + 1] = value[:, plan.block :].astype(BF16)


def forward_kernel(coupling, plan, place, *refs):
    refs = list(refs)
    last = coupling == plan.levels - 1
    solvers = take(refs, plan.n_col)
    pieces = solvers if coupling == 1 else views(plan, take(refs, 2))
    received = take(refs, plan.n_row)
    keep = refs.pop(0)
    if last:
        out = take(refs, plan.n_row)
    else:
        message, index_out = take(refs, 2)
    left, right, total, index, sem = take(refs, 5)
    if last:
        index_out, upper, back_left, back_right = refs
    decode(plan, place, pieces, index_out)
    copy = pltpu.make_async_copy(index_out, index, sem)
    copy.start()
    multiply_forward(plan, place, pieces, received, index, left, right, total, copy.wait)

    def coupled(u):
        return jnp.concatenate([total[2 * u], total[2 * u + 1]], axis=1)

    if not last:

        def write(piece, u, value):
            keep[u] = value
            message[u] = value.astype(BF16)

        level_forward(plan, place, coupling + 1, solvers, coupled, write)
        return
    back_left[...] = jnp.zeros_like(back_left)
    back_right[...] = jnp.zeros_like(back_right)

    def write_top(piece, u, value):
        value = apply_pair_transposed(piece[plan.inverse_rows(plan.levels), :], value, plan.block)
        keep[u] = value.astype(BF16)
        put_upper(plan, upper, u, value)

    level_forward(plan, place, plan.levels, solvers, coupled, write_top)
    multiply_backward(plan, place, pieces, index, upper, back_left, back_right, out)


def backward_kernel(level, plan, place, index, *refs):
    refs = list(refs)
    solvers = take(refs, plan.n_col)
    pieces = solvers if level == 2 else views(plan, take(refs, 2))
    shares = take(refs, plan.n_row)
    solved, keep = take(refs, 2)
    out = take(refs, plan.n_row)
    upper, left, right = refs
    left[...] = jnp.zeros_like(left)
    right[...] = jnp.zeros_like(right)
    back = add_up(shares)

    def write(u, value):
        keep[u] = value.astype(BF16)
        put_upper(plan, upper, u, value)

    level_backward(plan, place, level, solvers, lambda u: solved[u] - back(u), write)
    multiply_backward(plan, place, pieces, index, upper, left, right, out)


def leave_kernel(plan, place, *refs):
    refs = list(refs)
    pieces, shares = take(refs, plan.n_col), take(refs, plan.n_row)
    solved = refs.pop(0)
    above, out = take(refs, plan.levels - 1), refs
    back = add_up(shares)

    def write(u, value):
        for message in out:
            message[u] = value.astype(BF16)

    level_backward(plan, place, 1, pieces, lambda u: solved[u] - back(u), write)
    for chip, message in enumerate(out):
        base = (place[1] ^ (2 * chip)) // 2 * 2
        for core in range(2):
            for n, level in enumerate(above):
                message[plan.n_col + core * (plan.levels - 1) + n] = level[base + core]


def on_device(n_row, n_col, factor_tiles, tile_row, tile_col, right_sides, diag_inverse):
    plan = Plan(n_row, n_col, factor_tiles, right_sides)
    levels, chips = plan.levels, plan.chips
    place = jnp.stack([lax.axis_index("row"), lax.axis_index("col")]).astype(jnp.int32)

    def array(shape, kind=BF16):
        return jax.ShapeDtypeStruct(shape, kind)

    def over_row(value, m):
        return lax.ppermute(value, "row", [(i, i ^ m) for i in range(n_row)])

    def over_col(value, m):
        return lax.ppermute(value, "col", [(i, i ^ m) for i in range(n_col)])

    def exchange_row(values, order=1):
        got = {m: over_row(values[m], m) for m in range(1, n_row)[::order]}
        return [values[0]] + [got[m] for m in range(1, n_row)]

    def exchange_chips(values):
        return [values[0]] + [over_col(values[m], 2 * m) for m in range(1, chips)]

    def after(values, *others):
        return lax.optimization_barrier((values, others))[0]

    column = (plan.padded, plan.lanes)
    slices = (n_col, plan.slice, plan.lanes)
    dma = pltpu.SemaphoreType.DMA
    x0, message = call(
        plan, first_kernel, [array(column, F32), array(column)], (right_sides, diag_inverse),
        [pltpu.VMEM(right_sides.shape[1:], F32), pltpu.VMEM(diag_inverse.shape[1:], F32), dma((2,))],
        scalars=0, raw=(0, 1),
    )
    (message, place, tile_row, tile_col) = lax.optimization_barrier((message, place, tile_row, tile_col))
    received = exchange_row([message] * n_row)
    made = call(
        plan, pack_kernel,
        [array((plan.tile_rows, plan.lanes))]
        + [array((plan.first_rows(), plan.lanes))] * chips
        + [array((1, plan.inverse_at, plan.lanes)) for s in range(2, levels)],
        (place, tile_row, tile_col, factor_tiles, right_sides, diag_inverse),
        [pltpu.VMEM(factor_tiles.shape, BF16), pltpu.VMEM(right_sides.shape, F32),
         pltpu.VMEM(diag_inverse.shape, F32), pltpu.VMEM(column, BF16), dma((3,))],
        scalars=3, raw=(3, 4, 5),
    )
    pairs = made[0]
    payloads = [None, list(made[1 : 1 + chips])] + list(made[1 + chips :])

    def swap_cores(values):
        return [over_col(value, 1) for value in values]

    gathered = exchange_chips(after(payloads[1], received))
    near, late = gathered[:3], gathered[3:]
    keep, send = call(
        plan, near_forward_kernel, [array((chips,) + slices, F32), array((chips,) + slices)],
        [place, tile_row, tile_col, pairs] + received,
        [pltpu.VMEM((n_row * plan.rows_dev,) + column, BF16), pltpu.VMEM((n_row * plan.rows_dev,) + column, BF16),
         pltpu.VMEM((plan.own, plan.padded, plan.block), F32)],
        scalars=3,
    )
    near, send = lax.optimization_barrier((near, send))
    swapped, far = over_col(send, 1), swap_cores(near)
    swapped, near, far = lax.optimization_barrier((swapped, near, far))
    sums = call(plan, add_kernel, [array(slices, F32)] + [array(slices)] * (chips - 1), [keep, swapped], scalars=0)
    sums = exchange_chips(sums)
    first = near + late + far + swap_cores(late)
    solved, message = call(
        plan, enter_kernel, [array(slices, F32), array(slices)], [place] + first + sums
    )
    solved = [None, solved]

    index_shape = (max(8, n_col), 128)
    forward = [
        pltpu.VMEM((plan.blocks, plan.slice, plan.lanes), BF16),
        pltpu.VMEM((plan.blocks, plan.slice, plan.lanes), BF16),
        pltpu.VMEM((plan.own, plan.slice, plan.block), F32),
        pltpu.SMEM(index_shape, jnp.int32),
        dma(()),
    ]
    backward = [
        pltpu.VMEM((plan.own, plan.slice, plan.block), BF16),
        pltpu.VMEM((plan.blocks, plan.slice, plan.lanes), F32),
        pltpu.VMEM((plan.blocks, plan.slice, plan.lanes), F32),
    ]
    partial = [array(slices, F32)] + [array(slices)] * (n_row - 1)
    index = [None] * levels
    def double(held, step):
        other = over_col(held, 2 * step)
        return call(plan, join_kernel, [array((2 * step,) + held.shape[1:])], [held, other], scalars=0)[0]

    pieces = [None, []]
    for s in range(1, levels):
        if s + 1 < levels:
            held, step = double(after(payloads[s + 1], message), 1) if chips > 1 else payloads[s + 1], 2
        received = exchange_row([message] * n_row)
        if s + 1 < levels:
            held = after(held, received)
            while step < chips:
                held, step = double(held, step), 2 * step
        args = [place] + first + pieces[s] + received
        if s < levels - 1:
            value, message, index[s] = call(
                plan, functools.partial(forward_kernel, s),
                [array(slices, F32), array(slices), array(index_shape, jnp.int32)], args, forward,
            )
            solved.append(value)
            pieces.append([held, over_col(after(held, message), 1)])
        else:
            made = call(
                plan, functools.partial(forward_kernel, s), [array(slices)] + partial, args,
                forward + [pltpu.VMEM(index_shape, jnp.int32)] + backward,
            )
    results = [made[0]]
    shares = exchange_row(made[1:], -1)
    for level in range(levels - 1, 1, -1):
        made = call(
            plan, functools.partial(backward_kernel, level), [array(slices)] + partial,
            [place, index[level - 1]] + first + pieces[level - 1] + shares + [solved[level]],
            backward, scalars=2,
        )
        results.insert(0, made[0])
        shares = exchange_row(made[1:], -1)
    messages = call(
        plan, leave_kernel, [array((n_col + 2 * (levels - 1),) + slices[1:])] * chips,
        [place] + first + shares + [solved[1]] + results,
    )
    messages = exchange_chips(messages)
    messages = messages + swap_cores(messages)
    shares = call(
        plan, near_backward_kernel, [array(column, F32)] + [array(column)] * (n_row - 1),
        [place, tile_row, tile_col, pairs] + messages,
        [pltpu.VMEM((plan.own, plan.padded, plan.block), BF16),
         pltpu.VMEM((n_row * plan.rows_dev,) + column, F32), pltpu.VMEM((n_row * plan.rows_dev,) + column, F32)],
        scalars=3,
    )
    shares = exchange_row(shares, -1)
    return call(
        plan, last_kernel, [array(right_sides.shape, F32)], [place, diag_inverse, x0] + shares + messages,
        [pltpu.VMEM((levels,) + column, BF16)],
    )[0]


def solution(mesh):
    return jax.shard_map(
        functools.partial(on_device, mesh.shape["row"], mesh.shape["col"]),
        mesh=mesh,
        in_specs=(
            P(None, "row", None, "col"),
            P(None, "row", "col"),
            P(None, "row", "col"),
            P(None, ("col", "row"), None, None),
            P(None, None, ("col", "row")),
        ),
        out_specs=P(None, ("col", "row"), None, None),
        check_vma=False,
    )
```

```python
import functools

import jax
import jax.numpy as jnp
from jax import lax
from jax.experimental import pallas as pl
from jax.experimental.pallas import tpu as pltpu
from jax.sharding import PartitionSpec as P

BF16 = jnp.bfloat16
F32 = jnp.float32
NT = (((1,), (1,)), ((), ()))
TN = (((0,), (0,)), ((), ()))
SLICE_ROWS = 16


class Plan:
    def __init__(self, n_row, n_col, factor_tiles, right_sides):
        self.levels, self.tiles, self.block, _ = factor_tiles.shape
        self.rows_dev = right_sides.shape[1]
        self.vectors = right_sides.shape[3]
        self.n_row, self.n_col, self.chips = n_row, n_col, n_col // 2
        self.real = self.vectors // n_col
        self.slice = max(SLICE_ROWS, self.real)
        self.padded = self.slice * n_col
        self.lanes = self.rows_dev * self.block
        self.own = n_col * self.rows_dev
        self.blocks = n_row * self.own
        self.tile_rows = self.tiles // 2 * self.block
        self.inverse_at = self.tile_rows + 16
        self.vmem_bytes = (24 if n_col <= 8 else 48) << 20

    def payload_rows(self):
        return self.inverse_at + self.block

    def extra(self):
        return self.levels + self.block // self.slice

    def sources(self):
        return [2 * chip + core for core in range(2) for chip in range(self.chips)]


def call(plan, body, outs, args, scratch=(), scalars=1, raw=()):
    specs = [pl.BlockSpec(memory_space=pltpu.SMEM)] * scalars
    specs += [pl.BlockSpec(memory_space=pltpu.HBM if n in raw else pltpu.VMEM) for n in range(scalars, len(args))]
    return pl.pallas_call(
        functools.partial(body, plan),
        out_shape=outs,
        in_specs=specs,
        out_specs=[pl.BlockSpec(memory_space=pltpu.VMEM)] * len(outs),
        scratch_shapes=list(scratch),
        compiler_params=pltpu.CompilerParams(vmem_limit_bytes=plan.vmem_bytes),
    )(*args)


def row_order(values):
    values = list(values)
    return values[:1] + values[-1:] + values[1:-1]


def chip_order(values):
    values = list(values)
    return values[:1] + values[:0:-1]


def take(refs, count):
    return [refs.pop(0) for _ in range(count)]


def low_lanes(shape, half):
    return lax.broadcasted_iota(jnp.int32, shape, len(shape) - 1) < half


def split_rows(value):
    high = value.astype(BF16)
    return jnp.concatenate([high, (value - high.astype(F32)).astype(BF16)], axis=0)


def apply_pair(inverse, value, half):
    n = value.shape[0]
    both = jnp.concatenate([value, pltpu.roll(value, half, 1)], axis=0)[:, :half]
    out = jnp.dot(split_rows(both), inverse, preferred_element_type=F32)
    out = out[: 2 * n] + out[2 * n :]
    return jnp.where(low_lanes((n, 2 * half), half), out[:n], out[n:])


def apply_pair_transposed(inverse, value, half):
    n = value.shape[0]
    low = low_lanes(value.shape, half)
    both = jnp.concatenate([jnp.where(low, value, 0.0), jnp.where(low, 0.0, value)], axis=0)
    out = lax.dot_general(split_rows(both), inverse, NT, preferred_element_type=F32)
    out = out[: 2 * n] + out[2 * n :]
    return jnp.concatenate([out[:n], out[n:]], axis=1)


def pad_slices(plan, value, out):
    if plan.real == plan.slice:
        out[...] = value.astype(out.dtype)
        return
    out[...] = jnp.zeros_like(out)
    for c in range(plan.n_col):
        out[c * plan.slice : c * plan.slice + plan.real, :] = value[c * plan.real : (c + 1) * plan.real].astype(out.dtype)


def drop_padding(plan, value):
    if plan.real == plan.slice:
        return value
    return jnp.concatenate([value[c * plan.slice : c * plan.slice + plan.real] for c in range(plan.n_col)], axis=0)


def store_halves(left, right, at, value, half):
    low = low_lanes(value.shape, half)
    other = pltpu.roll(value, half, 1)
    left[2 * at] = jnp.where(low, value, 0.0).astype(BF16)
    right[2 * at] = jnp.where(low, 0.0, other).astype(BF16)
    left[2 * at + 1] = jnp.where(low, other, 0.0).astype(BF16)
    right[2 * at + 1] = jnp.where(low, 0.0, value).astype(BF16)


def join_halves(left, right, at, half):
    first = left[2 * at] + pltpu.roll(right[2 * at], half, 1)
    second = right[2 * at + 1] + pltpu.roll(left[2 * at + 1], half, 1)
    return jnp.where(low_lanes(first.shape, half), first, second)


def first_kernel(plan, sides, inverse, solved, message, sides_here, inverse_here, sems):
    copies = [
        pltpu.make_async_copy(sides.at[0], sides_here, sems.at[0]),
        pltpu.make_async_copy(inverse.at[0], inverse_here, sems.at[1]),
    ]
    for copy in copies:
        copy.start()
    for copy in copies:
        copy.wait()
    parts = [
        lax.dot_general(sides_here[b], inverse_here[:, b * plan.block : (b + 1) * plan.block], TN,
                        precision=lax.Precision.HIGHEST, preferred_element_type=F32)
        for b in range(plan.rows_dev)
    ]
    pad_slices(plan, jnp.concatenate(parts, axis=1), solved)
    message[...] = solved[...].astype(BF16)


def pack_kernel(plan, place, rows, cols, *refs):
    refs = list(refs)
    tiles, sides, inverse = take(refs, 3)
    first, side_slices, inverse_one = take(refs, 3)
    payloads = take(refs, plan.levels - 1)
    tiles_here, sides_here, inverse_here, sems = refs
    copies = [
        pltpu.make_async_copy(tiles, tiles_here, sems.at[0]),
        pltpu.make_async_copy(sides, sides_here, sems.at[1]),
        pltpu.make_async_copy(inverse, inverse_here, sems.at[2]),
    ]
    for copy in copies:
        copy.start()
    for copy in copies:
        copy.wait()
    half = plan.block
    lane = lax.broadcasted_iota(jnp.int32, (16, 128), 1)
    for coupling in range(plan.levels):
        target = payloads[coupling - 1].at[0] if coupling else first
        for k in range(plan.tiles // 2):
            pair = jnp.concatenate([tiles_here[coupling, 2 * k], tiles_here[coupling, 2 * k + 1]], axis=1)
            target[k * half : (k + 1) * half, :] = pair
        if coupling == 0:
            continue
        index = jnp.zeros((16, 128), F32)
        for t in range(plan.tiles):
            index = jnp.where(lane == t, rows[coupling, t, 0].astype(F32), index)
            index = jnp.where(lane == t + 64, cols[coupling, t, 0].astype(F32), index)
        target[plan.tile_rows : plan.inverse_at, :] = index.astype(BF16)
    inverse_one[...] = inverse_here[1].astype(BF16).reshape(inverse_one.shape)
    for level in range(1, plan.levels + 1):
        if level > 1:
            payloads[level - 2][0, plan.inverse_at :, :] = inverse_here[level].astype(BF16)
        both = jnp.concatenate([sides_here[level, b] for b in range(plan.rows_dev)], axis=0).T
        pad_slices(plan, both, side_slices.at[level - 1])


def near_forward_kernel(plan, place, rows, cols, pairs, *refs):
    refs = list(refs)
    received = take(refs, plan.n_row)
    side_slices, inverse_one = take(refs, 2)
    keep, keep_extra, send, left, right, total = refs
    half, width = plan.block, plan.slice
    for m in range(plan.n_row):
        store_halves(left, right, place[0] ^ m, received[m][...].astype(F32), half)
    total[...] = jnp.zeros_like(total)
    for k in range(plan.tiles // 2):
        pair = pairs[k * half : (k + 1) * half, :]
        vectors = jnp.concatenate([left[cols[0, 2 * k, 0]], right[cols[0, 2 * k + 1, 0]]], axis=0)
        product = lax.dot_general(vectors, pair, NT, preferred_element_type=F32)
        total[rows[0, 2 * k, 0]] += product[: plan.padded]
        total[rows[0, 2 * k + 1, 0]] += product[plan.padded :]
    for chip in range(plan.chips):
        for core, (out, extra, at) in enumerate(((keep, keep_extra, 0), (send, send, plan.n_col))):
            number = place[1] ^ (2 * chip + core)
            here = pl.ds(pl.multiple_of(number * width, 16), width)
            for u in range(plan.n_col):
                value = jnp.concatenate([total[2 * u, here, :], total[2 * u + 1, here, :]], axis=1)
                out[chip, u] = value.astype(out.dtype)
            for level in range(plan.levels):
                extra[chip, at + level] = side_slices[level, here, :]
            extra[chip, at + plan.levels : at + plan.extra()] = inverse_one[...]


def add_kernel(plan, place, keep, keep_extra, received, own, *out):
    here = plan.n_col + (place[1] & 1) * plan.extra()
    there = plan.n_col + (1 - (place[1] & 1)) * plan.extra()
    out = chip_order(out)
    own[...] = keep[0] + received[0, : plan.n_col].astype(F32)
    for chip in range(plan.chips):
        if chip:
            total = keep[chip] + received[chip, : plan.n_col].astype(F32)
            out[chip][: plan.n_col] = total.astype(BF16)
        out[chip][pl.ds(here, plan.extra())] = keep_extra[chip]
        out[chip][pl.ds(there, plan.extra())] = received[chip, plan.n_col :]


def near_backward_kernel(plan, place, rows, cols, pairs, *refs):
    refs = list(refs)
    received = take(refs, plan.n_col)
    out = row_order(take(refs, plan.n_row))
    upper, left, right = refs
    half, width = plan.block, plan.slice
    for piece, offset in zip(received, plan.sources()):
        here = pl.ds(pl.multiple_of((place[1] ^ offset) * width, 16), width)
        for u in range(plan.n_col):
            value = piece[u]
            upper[2 * u, here, :] = value[:, :half]
            upper[2 * u + 1, here, :] = value[:, half:]
    left[...] = jnp.zeros_like(left)
    right[...] = jnp.zeros_like(right)
    for k in range(plan.tiles // 2):
        pair = pairs[k * half : (k + 1) * half, :]
        vectors = jnp.concatenate([upper[rows[0, 2 * k, 0]], upper[rows[0, 2 * k + 1, 0]]], axis=0)
        product = jnp.dot(vectors, pair, preferred_element_type=F32)
        left[cols[0, 2 * k, 0]] += product[: plan.padded]
        right[cols[0, 2 * k + 1, 0]] += product[plan.padded :]
    for m in range(plan.n_row):
        out[m][...] = join_halves(left, right, place[0] ^ m, half).astype(out[m].dtype)


def last_kernel(plan, place, *refs):
    refs = list(refs)
    inverse, solved = take(refs, 2)
    shares = take(refs, plan.n_row)
    pieces = take(refs, plan.n_col)
    out, all_slices = refs
    half, width = plan.block, plan.slice
    core = place[1] & 1
    for piece, offset in zip(pieces, plan.sources()):
        here = pl.ds(pl.multiple_of((place[1] ^ offset) * width, 16), width)
        all_slices[0, here, :] = piece[place[1]]
        for n in range(1, plan.levels):
            all_slices[n, here, :] = piece[plan.n_col + core * (plan.levels - 1) + n - 1]
    for n in range(plan.levels):
        value = drop_padding(plan, all_slices[n].astype(F32)).T
        for b in range(plan.rows_dev):
            out[n + 1, b] = value[b * half : (b + 1) * half, :]
    back = shares[0][...].astype(F32)
    for share in shares[1:]:
        back = back + share[...].astype(F32)
    value = drop_padding(plan, solved[...] - back)
    for b in range(plan.rows_dev):
        cut = slice(b * half, (b + 1) * half)
        out[0, b] = lax.dot_general(inverse[0, :, cut], value[:, cut], NT,
                                    precision=lax.Precision.HIGHEST, preferred_element_type=F32)


def extras(plan, place, sums):
    core = place[1] & 1
    return [(sums[chip], plan.n_col + (core ^ other) * plan.extra()) for other in range(2) for chip in range(plan.chips)]


def inverse_of(plan, level, extra, piece):
    if level == 1:
        ref, at = extra
        return ref[pl.ds(at + plan.levels, plan.block // plan.slice)].reshape(plan.block, plan.lanes)
    return piece[plan.inverse_at :, :]


def level_forward(plan, place, level, sums, pieces, coupled, write):
    for extra, piece, offset in zip(extras(plan, place, sums), pieces, plan.sources()):
        u = place[1] ^ offset
        side = extra[0][extra[1] + level - 1].astype(F32)
        inverse = inverse_of(plan, level, extra, piece)
        write(inverse, u, apply_pair(inverse, side - coupled(u), plan.block))


def level_backward(plan, place, level, sums, pieces, value, write):
    for extra, piece, offset in zip(extras(plan, place, sums), pieces, plan.sources()):
        u = place[1] ^ offset
        write(u, apply_pair_transposed(inverse_of(plan, level, extra, piece), value(u), plan.block))


def join_kernel(plan, first, second, out):
    count = first.shape[0]
    out[:count] = first[...]
    out[count:] = second[...]


def views(plan, coupling, refs):
    order = list(range(plan.chips))
    if coupling % 2 == 0:
        bits = plan.chips.bit_length() - 1
        order = [sum(((chip >> n) & 1) << (bits - 1 - n) for n in range(bits)) for chip in order]
    return [ref.at[chip] for ref in refs for chip in order]


def add_up(refs):
    def total(u):
        value = refs[0][u].astype(F32)
        for ref in refs[1:]:
            value = value + ref[u].astype(F32)
        return value

    return total


def enter_kernel(plan, place, *refs):
    refs = list(refs)
    sums = take(refs, plan.chips + 1)
    solved, message = refs

    def write(inverse, u, value):
        solved[u] = value
        message[u] = value.astype(BF16)

    coupled = add_up([sums[0]] + sums[2:])
    level_forward(plan, place, 1, sums[1:], [None] * plan.n_col, coupled, write)


def decode(plan, place, pieces, index):
    lane = lax.broadcasted_iota(jnp.int32, (1, 128), 1)
    for p, offset in enumerate(plan.sources()):
        raw = pieces[p][plan.tile_rows : plan.inverse_at, :].astype(F32).astype(jnp.int32)[0:1]
        owner = raw // plan.rows_dev * plan.n_col + (place[1] ^ offset)
        col = owner * plan.rows_dev + raw % plan.rows_dev
        index[p : p + 1, :] = jnp.where(lane < 64, raw, col)


def multiply_forward(plan, place, pieces, received, index, left, right, total, ready):
    half, width = plan.block, plan.slice
    for m in range(plan.n_row):
        for u in range(plan.n_col):
            store_halves(left, right, (place[0] ^ m) * plan.n_col + u, received[m][u].astype(F32), half)
    total[...] = jnp.zeros_like(total)
    ready()
    for p in range(plan.n_col):
        for k in range(plan.tiles // 2):
            pair = pieces[p][k * half : (k + 1) * half, :]
            vectors = jnp.concatenate([left[index[p, 2 * k + 64]], right[index[p, 2 * k + 65]]], axis=0)
            product = lax.dot_general(vectors, pair, NT, preferred_element_type=F32)
            total[index[p, 2 * k]] += product[:width]
            total[index[p, 2 * k + 1]] += product[width:]


def multiply_backward(plan, place, pieces, index, upper, left, right, out):
    half, width = plan.block, plan.slice
    for p in range(plan.n_col):
        for k in range(plan.tiles // 2):
            pair = pieces[p][k * half : (k + 1) * half, :]
            vectors = jnp.concatenate([upper[index[p, 2 * k]], upper[index[p, 2 * k + 1]]], axis=0)
            product = jnp.dot(vectors, pair, preferred_element_type=F32)
            left[index[p, 2 * k + 64]] += product[:width]
            right[index[p, 2 * k + 65]] += product[width:]
    for m in range(plan.n_row):
        for u in range(plan.n_col):
            at = (place[0] ^ m) * plan.n_col + u
            out[m][u] = join_halves(left, right, at, half).astype(out[m].dtype)


def put_upper(plan, upper, u, value):
    upper[2 * u] = value[:, : plan.block].astype(BF16)
    upper[2 * u + 1] = value[:, plan.block :].astype(BF16)


def forward_kernel(coupling, plan, place, *refs):
    refs = list(refs)
    last = coupling == plan.levels - 1
    sums, pieces = take(refs, plan.chips), views(plan, coupling, take(refs, 2))
    received = take(refs, plan.n_row)
    keep = refs.pop(0)
    if last:
        out = row_order(take(refs, plan.n_row))
    else:
        message, index_out = take(refs, 2)
    left, right, total, index, sem = take(refs, 5)
    if last:
        index_out, upper, back_left, back_right = refs
    decode(plan, place, pieces, index_out)
    copy = pltpu.make_async_copy(index_out, index, sem)
    copy.start()
    multiply_forward(plan, place, pieces, received, index, left, right, total, copy.wait)

    def coupled(u):
        return jnp.concatenate([total[2 * u], total[2 * u + 1]], axis=1)

    if not last:

        def write(inverse, u, value):
            keep[u] = value
            message[u] = value.astype(BF16)

        level_forward(plan, place, coupling + 1, sums, pieces, coupled, write)
        return
    back_left[...] = jnp.zeros_like(back_left)
    back_right[...] = jnp.zeros_like(back_right)

    def write_top(inverse, u, value):
        value = apply_pair_transposed(inverse, value, plan.block)
        keep[u] = value.astype(BF16)
        put_upper(plan, upper, u, value)

    level_forward(plan, place, plan.levels, sums, pieces, coupled, write_top)
    multiply_backward(plan, place, pieces, index, upper, back_left, back_right, out)


def backward_kernel(level, plan, place, index, *refs):
    refs = list(refs)
    sums, pieces = take(refs, plan.chips), views(plan, level - 1, take(refs, 2))
    shares = take(refs, plan.n_row)
    solved, keep = take(refs, 2)
    out = row_order(take(refs, plan.n_row))
    upper, left, right = refs
    left[...] = jnp.zeros_like(left)
    right[...] = jnp.zeros_like(right)
    back = add_up(shares)

    def write(u, value):
        keep[u] = value.astype(BF16)
        put_upper(plan, upper, u, value)

    level_backward(plan, place, level, sums, pieces, lambda u: solved[u] - back(u), write)
    multiply_backward(plan, place, pieces, index, upper, left, right, out)


def leave_kernel(plan, place, *refs):
    refs = list(refs)
    sums, shares = take(refs, plan.chips), take(refs, plan.n_row)
    solved = refs.pop(0)
    above, out = take(refs, plan.levels - 1), chip_order(refs)
    back = add_up(shares)

    def write(u, value):
        for message in out:
            message[u] = value.astype(BF16)

    level_backward(plan, place, 1, sums, [None] * plan.n_col, lambda u: solved[u] - back(u), write)
    for chip, message in enumerate(out):
        base = (place[1] ^ (2 * chip)) // 2 * 2
        for core in range(2):
            for n, level in enumerate(above):
                message[plan.n_col + core * (plan.levels - 1) + n] = level[base + core]


def on_device(n_row, n_col, factor_tiles, tile_row, tile_col, right_sides, diag_inverse):
    plan = Plan(n_row, n_col, factor_tiles, right_sides)
    levels, chips = plan.levels, plan.chips
    place = jnp.stack([lax.axis_index("row"), lax.axis_index("col")]).astype(jnp.int32)

    def array(shape, kind=BF16):
        return jax.ShapeDtypeStruct(shape, kind)

    def over_row(value, m):
        return lax.ppermute(value, "row", [(i, i ^ m) for i in range(n_row)])

    def over_col(value, m):
        return lax.ppermute(value, "col", [(i, i ^ m) for i in range(n_col)])

    def exchange_row(values):
        got = {m: over_row(values[m], m) for m in [*range(2, n_row), 1]}
        return [values[0]] + [got[m] for m in range(1, n_row)]

    def exchange_chips(values):
        return [values[0]] + [over_col(values[m], 2 * m) for m in range(1, chips)]

    def after(values, *others):
        return lax.optimization_barrier((values, others))[0]

    column = (plan.padded, plan.lanes)
    slices = (n_col, plan.slice, plan.lanes)
    dma = pltpu.SemaphoreType.DMA
    x0, message = call(
        plan, first_kernel, [array(column, F32), array(column)], (right_sides, diag_inverse),
        [pltpu.VMEM(right_sides.shape[1:], F32), pltpu.VMEM(diag_inverse.shape[1:], F32), dma((2,))],
        scalars=0, raw=(0, 1),
    )
    (message, place, tile_row, tile_col) = lax.optimization_barrier((message, place, tile_row, tile_col))
    received = exchange_row([message] * n_row)
    pairs, side_slices, inverse_one, *held = call(
        plan, pack_kernel,
        [array((plan.tile_rows, plan.lanes)), array((levels,) + column),
         array((plan.block // plan.slice, plan.slice, plan.lanes))]
        + [array((1, plan.payload_rows(), plan.lanes))] * (levels - 1),
        (place, tile_row, tile_col, factor_tiles, right_sides, diag_inverse),
        [pltpu.VMEM(factor_tiles.shape, BF16), pltpu.VMEM(right_sides.shape, F32),
         pltpu.VMEM(diag_inverse.shape, F32), dma((3,))],
        scalars=3, raw=(3, 4, 5),
    )

    def join(held, other):
        shape = (2 * held.shape[0],) + held.shape[1:]
        return call(plan, join_kernel, [array(shape)], [held, other], scalars=0)[0]

    def step(held, coupling):
        bit = held.shape[0] if coupling % 2 else chips // 2 // held.shape[0]
        return held, over_col(held, 2 * bit)

    held = [step(value, s) for s, value in enumerate(after(held, received), 1)]
    keep, keep_extra, send = call(
        plan, near_forward_kernel,
        [array((chips,) + slices, F32), array((chips, plan.extra()) + slices[1:]),
         array((chips, n_col + plan.extra()) + slices[1:])],
        [place, tile_row, tile_col, pairs] + received + [side_slices, inverse_one],
        [pltpu.VMEM((n_row * plan.rows_dev,) + column, BF16), pltpu.VMEM((n_row * plan.rows_dev,) + column, BF16),
         pltpu.VMEM((plan.own, plan.padded, plan.block), F32)],
        scalars=3,
    )
    swapped = over_col(send, 1)
    made = call(
        plan, add_kernel, [array(slices, F32)] + [array((n_col + 2 * plan.extra(),) + slices[1:])] * chips,
        [place, keep, keep_extra, swapped],
    )
    own, sums = made[0], exchange_chips(chip_order(made[1:]))
    held = [join(*value) for value in after(held, sums)]
    if chips > 2:
        held = [step(value, s) for s, value in enumerate(held, 1)]
    solved, message = call(
        plan, enter_kernel, [array(slices, F32), array(slices)], [place, own] + sums
    )
    solved = [None, solved]

    index_shape = (max(8, n_col), 128)
    forward = [
        pltpu.VMEM((plan.blocks, plan.slice, plan.lanes), BF16),
        pltpu.VMEM((plan.blocks, plan.slice, plan.lanes), BF16),
        pltpu.VMEM((plan.own, plan.slice, plan.block), F32),
        pltpu.SMEM(index_shape, jnp.int32),
        dma(()),
    ]
    backward = [
        pltpu.VMEM((plan.own, plan.slice, plan.block), BF16),
        pltpu.VMEM((plan.blocks, plan.slice, plan.lanes), F32),
        pltpu.VMEM((plan.blocks, plan.slice, plan.lanes), F32),
    ]
    partial = [array(slices, F32)] + [array(slices)] * (n_row - 1)
    index = [None] * levels
    pieces = [None]
    for s in range(1, levels):
        received = exchange_row([message] * n_row)
        if s == 1 and chips > 2:
            received, held = lax.optimization_barrier((received, held))
            held = [join(*value) for value in held]
            while held[0].shape[0] < chips:
                held = [join(*step(value, n)) for n, value in enumerate(held, 1)]
        pieces.append([held[s - 1], over_col(held[s - 1], 1)])
        args = [place] + sums + pieces[s] + received
        if s < levels - 1:
            value, message, index[s] = call(
                plan, functools.partial(forward_kernel, s),
                [array(slices, F32), array(slices), array(index_shape, jnp.int32)], args, forward,
            )
            solved.append(value)
        else:
            made = call(
                plan, functools.partial(forward_kernel, s), [array(slices)] + partial, args,
                forward + [pltpu.VMEM(index_shape, jnp.int32)] + backward,
            )
    results = [made[0]]
    shares = exchange_row(row_order(made[1:]))
    for level in range(levels - 1, 1, -1):
        made = call(
            plan, functools.partial(backward_kernel, level), [array(slices)] + partial,
            [place, index[level - 1]] + sums + pieces[level - 1] + shares + [solved[level]],
            backward, scalars=2,
        )
        results.insert(0, made[0])
        shares = exchange_row(row_order(made[1:]))
    messages = call(
        plan, leave_kernel, [array((n_col + 2 * (levels - 1),) + slices[1:])] * chips,
        [place] + sums + shares + [solved[1]] + results,
    )
    messages = exchange_chips(chip_order(messages))
    messages = messages + [over_col(value, 1) for value in messages]
    shares = call(
        plan, near_backward_kernel, [array(column, F32)] + [array(column)] * (n_row - 1),
        [place, tile_row, tile_col, pairs] + messages,
        [pltpu.VMEM((plan.own, plan.padded, plan.block), BF16),
         pltpu.VMEM((n_row * plan.rows_dev,) + column, F32), pltpu.VMEM((n_row * plan.rows_dev,) + column, F32)],
        scalars=3,
    )
    shares = exchange_row(row_order(shares))
    return call(
        plan, last_kernel, [array(right_sides.shape, F32)], [place, diag_inverse, x0] + shares + messages,
        [pltpu.VMEM((levels,) + column, BF16)],
    )[0]


def solution(mesh):
    return jax.shard_map(
        functools.partial(on_device, mesh.shape["row"], mesh.shape["col"]),
        mesh=mesh,
        in_specs=(
            P(None, "row", None, "col"),
            P(None, "row", "col"),
            P(None, "row", "col"),
            P(None, ("col", "row"), None, None),
            P(None, None, ("col", "row")),
        ),
        out_specs=P(None, ("col", "row"), None, None),
        check_vma=False,
    )
```

```python
import functools

import jax
import jax.numpy as jnp
from jax import lax
from jax.experimental import pallas as pl
from jax.experimental.pallas import tpu as pltpu
from jax.sharding import PartitionSpec as P

BF16 = jnp.bfloat16
F32 = jnp.float32
NT = (((1,), (1,)), ((), ()))
TN = (((0,), (0,)), ((), ()))
SLICE_ROWS = 16


class Plan:
    def __init__(self, n_row, n_col, factor_tiles, right_sides):
        self.levels, self.tiles, self.block, _ = factor_tiles.shape
        self.rows_dev = right_sides.shape[1]
        self.vectors = right_sides.shape[3]
        self.n_row, self.n_col, self.chips = n_row, n_col, n_col // 2
        self.real = self.vectors // n_col
        self.slice = max(SLICE_ROWS, self.real)
        self.padded = self.slice * n_col
        self.lanes = self.rows_dev * self.block
        self.own = n_col * self.rows_dev
        self.blocks = n_row * self.own
        self.tile_rows = self.tiles // 2 * self.block
        self.inverse_at = self.tile_rows + 16
        self.vmem_bytes = (24 if n_col <= 8 else 48) << 20

    def payload_rows(self):
        return self.inverse_at + self.block

    def extra(self):
        return self.levels + self.block // self.slice

    def sources(self):
        return [2 * chip + core for core in range(2) for chip in range(self.chips)]


def call(plan, body, outs, args, scratch=(), scalars=0, raw=(), raw_out=False, aliases=None):
    def kernel(*refs):
        body(plan, (lax.axis_index("row"), lax.axis_index("col")), *refs)

    specs = [pl.BlockSpec(memory_space=pltpu.SMEM)] * scalars
    specs += [pl.BlockSpec(memory_space=pltpu.HBM if n in raw else pltpu.VMEM) for n in range(scalars, len(args))]
    return pl.pallas_call(
        kernel,
        out_shape=outs,
        in_specs=specs,
        out_specs=[pl.BlockSpec(memory_space=pltpu.HBM if raw_out else pltpu.VMEM)] * len(outs),
        scratch_shapes=list(scratch),
        input_output_aliases=aliases or {},
        compiler_params=pltpu.CompilerParams(vmem_limit_bytes=plan.vmem_bytes),
    )(*args)


def chip_order(values):
    return [values[0], *values[:0:-1]]


def take(refs, count):
    return [refs.pop(0) for _ in range(count)]


def low_lanes(shape, half):
    return lax.broadcasted_iota(jnp.int32, shape, len(shape) - 1) < half


def split_rows(value):
    high = value.astype(BF16)
    return jnp.concatenate([high, (value - high.astype(F32)).astype(BF16)], axis=0)


def apply_pair(inverse, value, half):
    n = value.shape[0]
    both = jnp.concatenate([value, pltpu.roll(value, half, 1)], axis=0)[:, :half]
    out = jnp.dot(split_rows(both), inverse, preferred_element_type=F32)
    out = out[: 2 * n] + out[2 * n :]
    return jnp.where(low_lanes((n, 2 * half), half), out[:n], out[n:])


def apply_pair_transposed(inverse, value, half):
    n = value.shape[0]
    low = low_lanes(value.shape, half)
    both = jnp.concatenate([jnp.where(low, value, 0.0), jnp.where(low, 0.0, value)], axis=0)
    out = lax.dot_general(split_rows(both), inverse, NT, preferred_element_type=F32)
    out = out[: 2 * n] + out[2 * n :]
    return jnp.concatenate([out[:n], out[n:]], axis=1)


def pad_slices(plan, value, out):
    if plan.real == plan.slice:
        out[...] = value.astype(out.dtype)
        return
    out[...] = jnp.zeros_like(out)
    for c in range(plan.n_col):
        out[c * plan.slice : c * plan.slice + plan.real, :] = value[c * plan.real : (c + 1) * plan.real].astype(out.dtype)


def drop_padding(plan, value):
    if plan.real == plan.slice:
        return value
    return jnp.concatenate([value[c * plan.slice : c * plan.slice + plan.real] for c in range(plan.n_col)], axis=0)


def store_halves(left, right, at, value, half):
    low = low_lanes(value.shape, half)
    other = pltpu.roll(value, half, 1)
    left[2 * at] = jnp.where(low, value, 0.0).astype(BF16)
    right[2 * at] = jnp.where(low, 0.0, other).astype(BF16)
    left[2 * at + 1] = jnp.where(low, other, 0.0).astype(BF16)
    right[2 * at + 1] = jnp.where(low, 0.0, value).astype(BF16)


def join_halves(left, right, at, half):
    first = left[2 * at] + pltpu.roll(right[2 * at], half, 1)
    second = right[2 * at + 1] + pltpu.roll(left[2 * at + 1], half, 1)
    return jnp.where(low_lanes(first.shape, half), first, second)


def first_kernel(plan, place, sides, inverse, solved, message, sides_here, inverse_here, sems):
    copies = [
        pltpu.make_async_copy(sides.at[0], sides_here, sems.at[0]),
        pltpu.make_async_copy(inverse.at[0], inverse_here, sems.at[1]),
    ]
    for copy in copies:
        copy.start()
    for copy in copies:
        copy.wait()
    parts = [
        lax.dot_general(sides_here[b], inverse_here[:, b * plan.block : (b + 1) * plan.block], TN,
                        precision=lax.Precision.HIGHEST, preferred_element_type=F32)
        for b in range(plan.rows_dev)
    ]
    pad_slices(plan, jnp.concatenate(parts, axis=1), solved)
    message[...] = solved[...].astype(BF16)


def pack_kernel(plan, place, rows, cols, *refs):
    refs = list(refs)
    tiles, sides, inverse = take(refs, 3)
    dense, side_slices, inverse_one = take(refs, 3)
    payloads = take(refs, plan.levels - 1)
    tiles_here, sides_here, inverse_here, sems = refs
    copies = [
        pltpu.make_async_copy(tiles, tiles_here, sems.at[0]),
        pltpu.make_async_copy(sides, sides_here, sems.at[1]),
        pltpu.make_async_copy(inverse, inverse_here, sems.at[2]),
    ]
    for copy in copies:
        copy.start()
    for copy in copies:
        copy.wait()
    half = plan.block
    lane = lax.broadcasted_iota(jnp.int32, (16, 128), 1)
    for coupling in range(plan.levels):
        if coupling == 0:
            dense[...] = jnp.zeros_like(dense)
            for t in range(plan.tiles):
                tile = tiles_here[0, t]
                col = cols[0, t, 0]
                both = jnp.concatenate([tile, tile], axis=1).astype(F32)
                here = (lax.broadcasted_iota(jnp.int32, both.shape, 1) // half) == col % 2
                at = pl.ds(pl.multiple_of(rows[0, t, 0] * half, half), half)
                dense[col // 2, at, :] += jnp.where(here, both, 0.0).astype(BF16)
            continue
        target = payloads[coupling - 1].at[0]
        for k in range(plan.tiles // 2):
            pair = jnp.concatenate([tiles_here[coupling, 2 * k], tiles_here[coupling, 2 * k + 1]], axis=1)
            target[k * half : (k + 1) * half, :] = pair
        index = jnp.zeros((16, 128), F32)
        for t in range(plan.tiles):
            index = jnp.where(lane == t, rows[coupling, t, 0].astype(F32), index)
            index = jnp.where(lane == t + 64, cols[coupling, t, 0].astype(F32), index)
        target[plan.tile_rows : plan.inverse_at, :] = index.astype(BF16)
    inverse_one[...] = inverse_here[1].astype(BF16).reshape(inverse_one.shape)
    for level in range(1, plan.levels + 1):
        if level > 1:
            payloads[level - 2][0, plan.inverse_at :, :] = inverse_here[level].astype(BF16)
        both = jnp.concatenate([sides_here[level, b] for b in range(plan.rows_dev)], axis=0).T
        pad_slices(plan, both, side_slices.at[level - 1])


def near_forward_kernel(plan, place, dense, *refs):
    refs = list(refs)
    received = take(refs, plan.n_row)
    side_slices, inverse_one = take(refs, 2)
    keep, keep_extra, send, total = refs
    width, lanes = plan.slice, plan.lanes
    vectors = jnp.concatenate([ref[...] for ref in received], axis=1)
    for u in range(0, plan.n_col, 2):
        matrix = [dense[place[0] ^ m, u * lanes : (u + 2) * lanes, :] for m in range(plan.n_row)]
        matrix = jnp.concatenate(matrix, axis=1)
        product = lax.dot_general(vectors, matrix, NT, preferred_element_type=F32)
        for n in range(2):
            total[u + n] = product[:, n * lanes : (n + 1) * lanes]
    for chip in range(plan.chips):
        for core, (out, extra, at) in enumerate(((keep, keep_extra, 0), (send, send, plan.n_col))):
            number = place[1] ^ (2 * chip + core)
            here = pl.ds(pl.multiple_of(number * width, 16), width)
            for u in range(plan.n_col):
                out[chip, u] = total[u, here, :].astype(out.dtype)
            for level in range(plan.levels):
                extra[chip, at + level] = side_slices[level, here, :]
            extra[chip, at + plan.levels : at + plan.extra()] = inverse_one[...]


def add_kernel(plan, place, keep, keep_extra, received, own, *out):
    here = plan.n_col + (place[1] & 1) * plan.extra()
    there = plan.n_col + (1 - (place[1] & 1)) * plan.extra()
    own[...] = keep[0] + received[0, : plan.n_col].astype(F32)
    for chip in range(plan.chips):
        if chip:
            total = keep[chip] + received[chip, : plan.n_col].astype(F32)
            out[chip][: plan.n_col] = total.astype(BF16)
        out[chip][pl.ds(here, plan.extra())] = keep_extra[chip]
        out[chip][pl.ds(there, plan.extra())] = received[chip, plan.n_col :]


def near_backward_kernel(plan, place, dense, *refs):
    refs = list(refs)
    received = take(refs, plan.n_col)
    out = take(refs, plan.n_row)
    (upper,) = refs
    width, lanes = plan.slice, plan.lanes
    for piece, offset in zip(received, plan.sources()):
        here = pl.ds(pl.multiple_of((place[1] ^ offset) * width, 16), width)
        for u in range(plan.n_col):
            upper[here, u * lanes : (u + 1) * lanes] = piece[u]
    vectors = upper[...]
    for m in range(0, plan.n_row, 2):
        matrix = jnp.concatenate([dense[place[0] ^ m], dense[place[0] ^ (m + 1)]], axis=1)
        product = jnp.dot(vectors, matrix, preferred_element_type=F32)
        for n in range(2):
            out[m + n][...] = product[:, n * lanes : (n + 1) * lanes].astype(out[m + n].dtype)


def upper_out_kernel(plan, place, *refs):
    refs = list(refs)
    pieces = take(refs, plan.n_col)
    out, all_slices, result, sem = refs
    half, width = plan.block, plan.slice
    core = place[1] & 1
    for piece, offset in zip(pieces, plan.sources()):
        here = pl.ds(pl.multiple_of((place[1] ^ offset) * width, 16), width)
        all_slices[0, here, :] = piece[place[1]]
        for n in range(1, plan.levels):
            all_slices[n, here, :] = piece[plan.n_col + core * (plan.levels - 1) + n - 1]
    for n in range(plan.levels):
        value = drop_padding(plan, all_slices[n].astype(F32)).T
        for b in range(plan.rows_dev):
            result[n, b] = value[b * half : (b + 1) * half, :]
    copy = pltpu.make_async_copy(result, out.at[1:], sem)
    copy.start()
    copy.wait()


def last_kernel(plan, place, inverse, solved, *refs):
    refs = list(refs)
    shares = take(refs, plan.n_row)
    _, out, result, sem = refs
    half = plan.block
    back = shares[0][...].astype(F32)
    for share in shares[1:]:
        back = back + share[...].astype(F32)
    value = drop_padding(plan, solved[...] - back)
    for b in range(plan.rows_dev):
        cut = slice(b * half, (b + 1) * half)
        result[b] = lax.dot_general(inverse[0, :, cut], value[:, cut], NT,
                                    precision=lax.Precision.HIGHEST, preferred_element_type=F32)
    copy = pltpu.make_async_copy(result, out.at[0], sem)
    copy.start()
    copy.wait()


def extras(plan, place, sums):
    core = place[1] & 1
    return [(sums[chip], plan.n_col + (core ^ other) * plan.extra()) for other in range(2) for chip in range(plan.chips)]


def inverse_of(plan, level, extra, piece):
    if level == 1:
        ref, at = extra
        return ref[pl.ds(at + plan.levels, plan.block // plan.slice)].reshape(plan.block, plan.lanes)
    return piece[plan.inverse_at :, :]


def level_forward(plan, place, level, sums, pieces, coupled, write):
    made = []
    for extra, piece, offset in zip(extras(plan, place, sums), pieces, plan.sources()):
        u = place[1] ^ offset
        side = extra[0][extra[1] + level - 1].astype(F32)
        inverse = inverse_of(plan, level, extra, piece)
        made.append((inverse, u, apply_pair(inverse, side - coupled(u), plan.block)))
    write(made)


def level_backward(plan, place, level, sums, pieces, value, write):
    made = []
    for extra, piece, offset in zip(extras(plan, place, sums), pieces, plan.sources()):
        u = place[1] ^ offset
        made.append((u, apply_pair_transposed(inverse_of(plan, level, extra, piece), value(u), plan.block)))
    for u, value in made:
        write(u, value)


def join_kernel(plan, place, first, second, out):
    count = first.shape[0]
    out[:count] = first[...]
    out[count:] = second[...]


def views(plan, coupling, refs):
    order = list(range(plan.chips))
    if coupling % 2 == 0:
        bits = plan.chips.bit_length() - 1
        order = [sum(((chip >> n) & 1) << (bits - 1 - n) for n in range(bits)) for chip in order]
    return [ref.at[chip] for ref in refs for chip in order]


def add_up(refs):
    def total(u):
        value = refs[0][u].astype(F32)
        for ref in refs[1:]:
            value = value + ref[u].astype(F32)
        return value

    return total


def enter_kernel(plan, place, *refs):
    refs = list(refs)
    own, sums = refs.pop(0), chip_order(take(refs, plan.chips))
    solved, message = refs

    def write(made):
        for _, u, value in made:
            solved[u] = value
            message[u] = value.astype(BF16)

    coupled = add_up([own] + sums[1:])
    level_forward(plan, place, 1, sums, [None] * plan.n_col, coupled, write)


def decode(plan, place, pieces, index):
    lane = lax.broadcasted_iota(jnp.int32, (1, 128), 1)
    for p, offset in enumerate(plan.sources()):
        raw = pieces[p][plan.tile_rows : plan.inverse_at, :].astype(F32).astype(jnp.int32)[0:1]
        owner = raw // plan.rows_dev * plan.n_col + (place[1] ^ offset)
        col = owner * plan.rows_dev + raw % plan.rows_dev
        index[p : p + 1, :] = jnp.where(lane < 64, raw, col)


def multiply_forward(plan, place, pieces, received, index, left, right, total, ready):
    half, width = plan.block, plan.slice
    for m in range(plan.n_row):
        for u in range(plan.n_col):
            store_halves(left, right, (place[0] ^ m) * plan.n_col + u, received[m][u].astype(F32), half)
    total[...] = jnp.zeros_like(total)
    ready()
    for p in range(plan.n_col):
        for k in range(plan.tiles // 2):
            pair = pieces[p][k * half : (k + 1) * half, :]
            vectors = jnp.concatenate([left[index[p, 2 * k + 64]], right[index[p, 2 * k + 65]]], axis=0)
            product = lax.dot_general(vectors, pair, NT, preferred_element_type=F32)
            total[index[p, 2 * k]] += product[:width]
            total[index[p, 2 * k + 1]] += product[width:]


def multiply_backward(plan, place, pieces, index, upper, left, right, out):
    half, width = plan.block, plan.slice
    for p in range(plan.n_col):
        for k in range(plan.tiles // 2):
            pair = pieces[p][k * half : (k + 1) * half, :]
            vectors = jnp.concatenate([upper[index[p, 2 * k]], upper[index[p, 2 * k + 1]]], axis=0)
            product = jnp.dot(vectors, pair, preferred_element_type=F32)
            left[index[p, 2 * k + 64]] += product[:width]
            right[index[p, 2 * k + 65]] += product[width:]
    for m in range(plan.n_row):
        for u in range(plan.n_col):
            at = (place[0] ^ m) * plan.n_col + u
            out[m][u] = join_halves(left, right, at, half).astype(out[m].dtype)


def put_upper(plan, upper, u, value):
    upper[2 * u] = value[:, : plan.block].astype(BF16)
    upper[2 * u + 1] = value[:, plan.block :].astype(BF16)


def forward_kernel(coupling, plan, place, *refs):
    refs = list(refs)
    last = coupling == plan.levels - 1
    sums, pieces = chip_order(take(refs, plan.chips)), views(plan, coupling, take(refs, 2))
    received = take(refs, plan.n_row)
    keep = refs.pop(0)
    if last:
        out = take(refs, plan.n_row)
    else:
        message, index_out = take(refs, 2)
    left, right, total, index, sem = take(refs, 5)
    if last:
        index_out, upper, back_left, back_right = refs
    decode(plan, place, pieces, index_out)
    copy = pltpu.make_async_copy(index_out, index, sem)
    copy.start()
    multiply_forward(plan, place, pieces, received, index, left, right, total, copy.wait)

    def coupled(u):
        return jnp.concatenate([total[2 * u], total[2 * u + 1]], axis=1)

    if not last:

        def write(made):
            for _, u, value in made:
                keep[u] = value
                message[u] = value.astype(BF16)

        level_forward(plan, place, coupling + 1, sums, pieces, coupled, write)
        return
    back_left[...] = jnp.zeros_like(back_left)
    back_right[...] = jnp.zeros_like(back_right)

    def write_top(made):
        made = [(u, apply_pair_transposed(inverse, value, plan.block)) for inverse, u, value in made]
        for u, value in made:
            keep[u] = value.astype(BF16)
            put_upper(plan, upper, u, value)

    level_forward(plan, place, plan.levels, sums, pieces, coupled, write_top)
    multiply_backward(plan, place, pieces, index, upper, back_left, back_right, out)


def backward_kernel(level, plan, place, index_here, *refs):
    refs = list(refs)
    sums, pieces = chip_order(take(refs, plan.chips)), views(plan, level - 1, take(refs, 2))
    shares = take(refs, plan.n_row)
    solved, keep = take(refs, 2)
    out = take(refs, plan.n_row)
    upper, left, right, index, sem = refs
    copy = pltpu.make_async_copy(index_here, index, sem)
    copy.start()
    left[...] = jnp.zeros_like(left)
    right[...] = jnp.zeros_like(right)
    back = add_up(shares)

    def write(u, value):
        keep[u] = value.astype(BF16)
        put_upper(plan, upper, u, value)

    level_backward(plan, place, level, sums, pieces, lambda u: solved[u] - back(u), write)
    copy.wait()
    multiply_backward(plan, place, pieces, index, upper, left, right, out)


def leave_kernel(plan, place, *refs):
    refs = list(refs)
    sums, shares = chip_order(take(refs, plan.chips)), take(refs, plan.n_row)
    solved = refs.pop(0)
    above, out = take(refs, plan.levels - 1), refs
    back = add_up(shares)

    def write(u, value):
        for message in out:
            message[u] = value.astype(BF16)

    level_backward(plan, place, 1, sums, [None] * plan.n_col, lambda u: solved[u] - back(u), write)
    for chip, message in enumerate(out):
        base = (place[1] ^ (2 * chip)) // 2 * 2
        for core in range(2):
            for n, level in enumerate(above):
                message[plan.n_col + core * (plan.levels - 1) + n] = level[base + core]


def on_device(n_row, n_col, factor_tiles, tile_row, tile_col, right_sides, diag_inverse):
    plan = Plan(n_row, n_col, factor_tiles, right_sides)
    levels, chips = plan.levels, plan.chips

    def array(shape, kind=BF16):
        return jax.ShapeDtypeStruct(shape, kind)

    def over_row(value, m):
        return lax.ppermute(value, "row", [(i, i ^ m) for i in range(n_row)])

    def over_col(value, m):
        return lax.ppermute(value, "col", [(i, i ^ m) for i in range(n_col)])

    def gather_row(value):
        return [value] + [over_row(value, m) for m in range(1, n_row)]

    def exchange_row(values):
        return [values[0]] + [over_row(values[m], m) for m in range(n_row - 1, 0, -1)]

    def exchange_chips(values):
        return [values[0]] + [over_col(values[m], 2 * m) for m in range(1, chips)]

    def after(values, *others):
        return lax.optimization_barrier((values, others))[0]

    column = (plan.padded, plan.lanes)
    slices = (n_col, plan.slice, plan.lanes)
    dma = pltpu.SemaphoreType.DMA
    x0, message = call(
        plan, first_kernel, [array(column, F32), array(column)], (right_sides, diag_inverse),
        [pltpu.VMEM(right_sides.shape[1:], F32), pltpu.VMEM(diag_inverse.shape[1:], F32), dma((2,))],
        raw=(0, 1),
    )
    message, tile_row, tile_col = lax.optimization_barrier((message, tile_row, tile_col))
    received = gather_row(message)
    dense, side_slices, inverse_one, *held = call(
        plan, pack_kernel,
        [array((n_row, plan.own * plan.block, plan.lanes)), array((levels,) + column),
         array((plan.block // plan.slice, plan.slice, plan.lanes))]
        + [array((1, plan.payload_rows(), plan.lanes))] * (levels - 1),
        (tile_row, tile_col, factor_tiles, right_sides, diag_inverse),
        [pltpu.VMEM(factor_tiles.shape, BF16), pltpu.VMEM(right_sides.shape, F32),
         pltpu.VMEM(diag_inverse.shape, F32), dma((3,))],
        scalars=2, raw=(2, 3, 4),
    )

    def join(held, other):
        shape = (2 * held.shape[0],) + held.shape[1:]
        return call(plan, join_kernel, [array(shape)], [held, other])[0]

    def step(held, coupling):
        bit = held.shape[0] if coupling % 2 else chips // 2 // held.shape[0]
        return held, over_col(held, 2 * bit)

    held = [step(value, s) for s, value in enumerate(after(held, received), 1)]
    keep, keep_extra, send = call(
        plan, near_forward_kernel,
        [array((chips,) + slices, F32), array((chips, plan.extra()) + slices[1:]),
         array((chips, n_col + plan.extra()) + slices[1:])],
        [dense] + received + [side_slices, inverse_one],
        [pltpu.VMEM((n_col,) + column, F32)],
    )
    swapped = over_col(send, 1)
    made = call(
        plan, add_kernel, [array(slices, F32)] + [array((n_col + 2 * plan.extra(),) + slices[1:])] * chips,
        [keep, keep_extra, swapped],
    )
    own, sums = made[0], exchange_chips(made[1:])
    held = [join(*value) for value in after(held, sums)]
    if chips > 2:
        held = [step(value, s) for s, value in enumerate(held, 1)]
    solved, message = call(
        plan, enter_kernel, [array(slices, F32), array(slices)], [own] + chip_order(sums)
    )
    solved = [None, solved]

    index_shape = (max(8, n_col), 128)
    forward = [
        pltpu.VMEM((plan.blocks, plan.slice, plan.lanes), BF16),
        pltpu.VMEM((plan.blocks, plan.slice, plan.lanes), BF16),
        pltpu.VMEM((plan.own, plan.slice, plan.block), F32),
        pltpu.SMEM(index_shape, jnp.int32),
        dma(()),
    ]
    backward = [
        pltpu.VMEM((plan.own, plan.slice, plan.block), BF16),
        pltpu.VMEM((plan.blocks, plan.slice, plan.lanes), F32),
        pltpu.VMEM((plan.blocks, plan.slice, plan.lanes), F32),
    ]
    partial = [array(slices, F32)] + [array(slices)] * (n_row - 1)
    index = [None] * levels
    pieces = [None]
    for s in range(1, levels):
        received = gather_row(message)
        if s == 1 and chips > 2:
            received, held = lax.optimization_barrier((received, held))
            held = [join(*value) for value in held]
            while held[0].shape[0] < chips:
                held = [join(*step(value, n)) for n, value in enumerate(held, 1)]
        pieces.append([held[s - 1], over_col(held[s - 1], 1)])
        args = chip_order(sums) + pieces[s] + received
        if s < levels - 1:
            value, message, index[s] = call(
                plan, functools.partial(forward_kernel, s),
                [array(slices, F32), array(slices), array(index_shape, jnp.int32)], args, forward,
            )
            solved.append(value)
        else:
            made = call(
                plan, functools.partial(forward_kernel, s), [array(slices)] + partial, args,
                forward + [pltpu.VMEM(index_shape, jnp.int32)] + backward,
            )
    results = [made[0]]
    shares = exchange_row(made[1:])
    for level in range(levels - 1, 1, -1):
        made = call(
            plan, functools.partial(backward_kernel, level), [array(slices)] + partial,
            [index[level - 1]] + chip_order(sums) + pieces[level - 1] + shares + [solved[level]],
            backward + [pltpu.SMEM(index_shape, jnp.int32), dma(())],
        )
        results.insert(0, made[0])
        shares = exchange_row(made[1:])
    messages = call(
        plan, leave_kernel, [array((n_col + 2 * (levels - 1),) + slices[1:])] * chips,
        chip_order(sums) + shares + [solved[1]] + results,
    )
    messages = exchange_chips(messages)
    messages = messages + [over_col(value, 1) for value in messages]
    shares = call(
        plan, near_backward_kernel, [array(column, F32)] + [array(column)] * (n_row - 1), [dense] + messages,
        [pltpu.VMEM((plan.padded, n_col * plan.lanes), BF16)],
    )
    shares = exchange_row(shares)
    result = array(right_sides.shape, F32)
    upper = call(
        plan, upper_out_kernel, [result], messages,
        [pltpu.VMEM((levels,) + column, BF16), pltpu.VMEM((levels,) + right_sides.shape[1:], F32), dma(())],
        raw_out=True,
    )[0]
    args = [diag_inverse, x0] + shares + [upper]
    return call(
        plan, last_kernel, [result], args, [pltpu.VMEM(right_sides.shape[1:], F32), dma(())],
        raw=(len(args) - 1,), raw_out=True, aliases={len(args) - 1: 0},
    )[0]


def solution(mesh):
    return jax.shard_map(
        functools.partial(on_device, mesh.shape["row"], mesh.shape["col"]),
        mesh=mesh,
        in_specs=(
            P(None, "row", None, "col"),
            P(None, "row", "col"),
            P(None, "row", "col"),
            P(None, ("col", "row"), None, None),
            P(None, None, ("col", "row")),
        ),
        out_specs=P(None, ("col", "row"), None, None),
        check_vma=False,
    )
```

```python
import functools

import jax
import jax.numpy as jnp
from jax import lax
from jax.experimental import pallas as pl
from jax.experimental.pallas import tpu as pltpu
from jax.sharding import PartitionSpec as P

BF16 = jnp.bfloat16
F32 = jnp.float32
NT = (((1,), (1,)), ((), ()))
TN = (((0,), (0,)), ((), ()))
SLICE_ROWS = 16


class Plan:
    def __init__(self, n_row, n_col, factor_tiles, right_sides):
        self.levels, self.tiles, self.block, _ = factor_tiles.shape
        self.rows_dev = right_sides.shape[1]
        self.vectors = right_sides.shape[3]
        self.n_row, self.n_col, self.chips = n_row, n_col, n_col // 2
        self.real = self.vectors // n_col
        self.slice = max(SLICE_ROWS, self.real)
        self.padded = self.slice * n_col
        self.lanes = self.rows_dev * self.block
        self.own = n_col * self.rows_dev
        self.blocks = n_row * self.own
        self.tile_rows = self.tiles // 2 * self.block
        self.inverse_at = self.tile_rows + 16
        self.vmem_bytes = (24 if n_col <= 8 else 48) << 20

    def payload_rows(self):
        return self.inverse_at + self.block

    def extra(self):
        return self.levels + self.block // self.slice

    def sources(self):
        return [2 * chip + core for core in range(2) for chip in range(self.chips)]


def call(plan, body, outs, args, scratch=(), scalars=0, raw=(), raw_out=False, aliases=None):
    def kernel(*refs):
        body(plan, (lax.axis_index("row"), lax.axis_index("col")), *refs)

    specs = [pl.BlockSpec(memory_space=pltpu.SMEM)] * scalars
    specs += [pl.BlockSpec(memory_space=pltpu.HBM if n in raw else pltpu.VMEM) for n in range(scalars, len(args))]
    return pl.pallas_call(
        kernel,
        out_shape=outs,
        in_specs=specs,
        out_specs=[pl.BlockSpec(memory_space=pltpu.HBM if raw_out else pltpu.VMEM)] * len(outs),
        scratch_shapes=list(scratch),
        input_output_aliases=aliases or {},
        compiler_params=pltpu.CompilerParams(vmem_limit_bytes=plan.vmem_bytes),
    )(*args)


def chip_order(values):
    return [values[0], *values[:0:-1]]


def take(refs, count):
    return [refs.pop(0) for _ in range(count)]


def low_lanes(shape, half):
    return lax.broadcasted_iota(jnp.int32, shape, len(shape) - 1) < half


def split_rows(value):
    high = value.astype(BF16)
    return jnp.concatenate([high, (value - high.astype(F32)).astype(BF16)], axis=0)


def apply_pair(inverse, value, half):
    n = value.shape[0]
    both = jnp.concatenate([value, pltpu.roll(value, half, 1)], axis=0)[:, :half]
    out = jnp.dot(split_rows(both), inverse, preferred_element_type=F32)
    out = out[: 2 * n] + out[2 * n :]
    return jnp.where(low_lanes((n, 2 * half), half), out[:n], out[n:])


def apply_pair_transposed(inverse, value, half):
    n = value.shape[0]
    low = low_lanes(value.shape, half)
    both = jnp.concatenate([jnp.where(low, value, 0.0), jnp.where(low, 0.0, value)], axis=0)
    out = lax.dot_general(split_rows(both), inverse, NT, preferred_element_type=F32)
    out = out[: 2 * n] + out[2 * n :]
    return jnp.concatenate([out[:n], out[n:]], axis=1)


def pad_slices(plan, value, out):
    if plan.real == plan.slice:
        out[...] = value.astype(out.dtype)
        return
    out[...] = jnp.zeros_like(out)
    for c in range(plan.n_col):
        out[c * plan.slice : c * plan.slice + plan.real, :] = value[c * plan.real : (c + 1) * plan.real].astype(out.dtype)


def drop_padding(plan, value):
    if plan.real == plan.slice:
        return value
    return jnp.concatenate([value[c * plan.slice : c * plan.slice + plan.real] for c in range(plan.n_col)], axis=0)


def store_halves(left, right, at, value, half):
    low = low_lanes(value.shape, half)
    other = pltpu.roll(value, half, 1)
    left[2 * at] = jnp.where(low, value, 0.0).astype(BF16)
    right[2 * at] = jnp.where(low, 0.0, other).astype(BF16)
    left[2 * at + 1] = jnp.where(low, other, 0.0).astype(BF16)
    right[2 * at + 1] = jnp.where(low, 0.0, value).astype(BF16)


def join_halves(left, right, at, half):
    first = left[2 * at] + pltpu.roll(right[2 * at], half, 1)
    second = right[2 * at + 1] + pltpu.roll(left[2 * at + 1], half, 1)
    return jnp.where(low_lanes(first.shape, half), first, second)


def first_kernel(plan, place, sides, inverse, solved, message):
    parts = [
        lax.dot_general(sides[0, b], inverse[0, :, b * plan.block : (b + 1) * plan.block], TN,
                        precision=lax.Precision.HIGHEST, preferred_element_type=F32)
        for b in range(plan.rows_dev)
    ]
    pad_slices(plan, jnp.concatenate(parts, axis=1), solved)
    message[...] = solved[...].astype(BF16)


def pack_kernel(plan, place, rows, cols, *refs):
    refs = list(refs)
    tiles, sides, inverse = take(refs, 3)
    dense, side_slices, inverse_one = take(refs, 3)
    payloads = take(refs, plan.levels - 1)
    half = plan.block
    lane = lax.broadcasted_iota(jnp.int32, (16, 128), 1)
    for coupling in range(plan.levels):
        if coupling == 0:
            dense[...] = jnp.zeros_like(dense)
            for t in range(plan.tiles):
                tile = tiles[0, t]
                col = cols[0, 0, t]
                both = jnp.concatenate([tile, tile], axis=1).astype(F32)
                here = (lax.broadcasted_iota(jnp.int32, both.shape, 1) // half) == col % 2
                at = pl.ds(pl.multiple_of(rows[0, 0, t] * half, half), half)
                dense[col // 2, at, :] += jnp.where(here, both, 0.0).astype(BF16)
            continue
        target = payloads[coupling - 1].at[0]
        for k in range(plan.tiles // 2):
            pair = jnp.concatenate([tiles[coupling, 2 * k], tiles[coupling, 2 * k + 1]], axis=1)
            target[k * half : (k + 1) * half, :] = pair
        index = jnp.zeros((16, 128), F32)
        for t in range(plan.tiles):
            index = jnp.where(lane == t, rows[coupling, 0, t].astype(F32), index)
            index = jnp.where(lane == t + 64, cols[coupling, 0, t].astype(F32), index)
        target[plan.tile_rows : plan.inverse_at, :] = index.astype(BF16)
    inverse_one[...] = inverse[1].astype(BF16).reshape(inverse_one.shape)
    for level in range(1, plan.levels + 1):
        if level > 1:
            payloads[level - 2][0, plan.inverse_at :, :] = inverse[level].astype(BF16)
        both = jnp.concatenate([sides[level, b] for b in range(plan.rows_dev)], axis=0).T
        pad_slices(plan, both, side_slices.at[level - 1])


def near_forward_kernel(plan, place, dense, *refs):
    refs = list(refs)
    received = take(refs, plan.n_row)
    side_slices, inverse_one = take(refs, 2)
    keep, keep_extra, send, total = refs
    width, lanes = plan.slice, plan.lanes
    vectors = jnp.concatenate([ref[...] for ref in received], axis=1)
    for u in range(0, plan.n_col, 2):
        matrix = [dense[place[0] ^ m, u * lanes : (u + 2) * lanes, :] for m in range(plan.n_row)]
        matrix = jnp.concatenate(matrix, axis=1)
        product = lax.dot_general(vectors, matrix, NT, preferred_element_type=F32)
        for n in range(2):
            total[u + n] = product[:, n * lanes : (n + 1) * lanes]
    for chip in range(plan.chips):
        for core, (out, extra, at) in enumerate(((keep, keep_extra, 0), (send, send, plan.n_col))):
            number = place[1] ^ (2 * chip + core)
            here = pl.ds(pl.multiple_of(number * width, 16), width)
            for u in range(plan.n_col):
                out[chip, u] = total[u, here, :].astype(out.dtype)
            for level in range(plan.levels):
                extra[chip, at + level] = side_slices[level, here, :]
            extra[chip, at + plan.levels : at + plan.extra()] = inverse_one[...]


def add_kernel(plan, place, keep, keep_extra, received, own, *out):
    here = plan.n_col + (place[1] & 1) * plan.extra()
    there = plan.n_col + (1 - (place[1] & 1)) * plan.extra()
    own[...] = keep[0] + received[0, : plan.n_col].astype(F32)
    for chip in range(plan.chips):
        if chip:
            total = keep[chip] + received[chip, : plan.n_col].astype(F32)
            out[chip][: plan.n_col] = total.astype(BF16)
        out[chip][pl.ds(here, plan.extra())] = keep_extra[chip]
        out[chip][pl.ds(there, plan.extra())] = received[chip, plan.n_col :]


def near_backward_kernel(plan, place, dense, *refs):
    refs = list(refs)
    received = take(refs, plan.n_col)
    out = take(refs, plan.n_row)
    (upper,) = refs
    width, lanes = plan.slice, plan.lanes
    for piece, offset in zip(received, plan.sources()):
        here = pl.ds(pl.multiple_of((place[1] ^ offset) * width, 16), width)
        for u in range(plan.n_col):
            upper[here, u * lanes : (u + 1) * lanes] = piece[u]
    vectors = upper[...]
    for m in range(0, plan.n_row, 2):
        matrix = jnp.concatenate([dense[place[0] ^ m], dense[place[0] ^ (m + 1)]], axis=1)
        product = jnp.dot(vectors, matrix, preferred_element_type=F32)
        for n in range(2):
            out[m + n][...] = product[:, n * lanes : (n + 1) * lanes].astype(out[m + n].dtype)


def upper_out_kernel(plan, place, *refs):
    refs = list(refs)
    pieces = take(refs, plan.n_col)
    out, all_slices, result, sem = refs
    half, width = plan.block, plan.slice
    core = place[1] & 1
    for piece, offset in zip(pieces, plan.sources()):
        here = pl.ds(pl.multiple_of((place[1] ^ offset) * width, 16), width)
        all_slices[0, here, :] = piece[place[1]]
        for n in range(1, plan.levels):
            all_slices[n, here, :] = piece[plan.n_col + core * (plan.levels - 1) + n - 1]
    for n in range(plan.levels):
        value = drop_padding(plan, all_slices[n].astype(F32)).T
        for b in range(plan.rows_dev):
            result[n, b] = value[b * half : (b + 1) * half, :]
    copy = pltpu.make_async_copy(result, out.at[1:], sem)
    copy.start()
    copy.wait()


def last_kernel(plan, place, inverse, solved, *refs):
    refs = list(refs)
    shares = take(refs, plan.n_row)
    _, out, result, sem = refs
    half = plan.block
    back = shares[0][...].astype(F32)
    for share in shares[1:]:
        back = back + share[...].astype(F32)
    value = drop_padding(plan, solved[...] - back)
    for b in range(plan.rows_dev):
        cut = slice(b * half, (b + 1) * half)
        result[b] = lax.dot_general(inverse[0, :, cut], value[:, cut], NT,
                                    precision=lax.Precision.HIGHEST, preferred_element_type=F32)
    copy = pltpu.make_async_copy(result, out.at[0], sem)
    copy.start()
    copy.wait()


def extras(plan, place, sums):
    core = place[1] & 1
    return [(sums[chip], plan.n_col + (core ^ other) * plan.extra()) for other in range(2) for chip in range(plan.chips)]


def inverse_of(plan, level, extra, piece):
    if level == 1:
        ref, at = extra
        return ref[pl.ds(at + plan.levels, plan.block // plan.slice)].reshape(plan.block, plan.lanes)
    return piece[plan.inverse_at :, :]


def level_forward(plan, place, level, sums, pieces, coupled, write):
    made = []
    for extra, piece, offset in zip(extras(plan, place, sums), pieces, plan.sources()):
        u = place[1] ^ offset
        side = extra[0][extra[1] + level - 1].astype(F32)
        inverse = inverse_of(plan, level, extra, piece)
        made.append((inverse, u, apply_pair(inverse, side - coupled(u), plan.block)))
    write(made)


def level_backward(plan, place, level, sums, pieces, value, write):
    made = []
    for extra, piece, offset in zip(extras(plan, place, sums), pieces, plan.sources()):
        u = place[1] ^ offset
        made.append((u, apply_pair_transposed(inverse_of(plan, level, extra, piece), value(u), plan.block)))
    for u, value in made:
        write(u, value)


def join_kernel(plan, place, first, second, out):
    count = first.shape[0]
    out[:count] = first[...]
    out[count:] = second[...]


def views(plan, coupling, refs):
    order = list(range(plan.chips))
    if coupling % 2 == 0:
        bits = plan.chips.bit_length() - 1
        order = [sum(((chip >> n) & 1) << (bits - 1 - n) for n in range(bits)) for chip in order]
    return [ref.at[chip] for ref in refs for chip in order]


def add_up(refs):
    def total(u):
        value = refs[0][u].astype(F32)
        for ref in refs[1:]:
            value = value + ref[u].astype(F32)
        return value

    return total


def enter_kernel(plan, place, *refs):
    refs = list(refs)
    own, sums = refs.pop(0), chip_order(take(refs, plan.chips))
    solved, message = refs

    def write(made):
        for _, u, value in made:
            solved[u] = value
            message[u] = value.astype(BF16)

    coupled = add_up([own] + sums[1:])
    level_forward(plan, place, 1, sums, [None] * plan.n_col, coupled, write)


def decode(plan, place, core, pieces):
    def reader(row, col):
        return lambda tile: (row[0, tile], col[0, tile + 64])

    readers = []
    for chip, piece in enumerate(pieces):
        raw = piece[plan.tile_rows : plan.inverse_at, :].astype(F32).astype(jnp.int32)[0:1]
        owner = raw // plan.rows_dev * plan.n_col + (place[1] ^ (2 * chip + core))
        readers.append(reader(raw, owner * plan.rows_dev + raw % plan.rows_dev))
    return readers


def multiply_forward(plan, place, core, pieces, left, right, totals):
    half, width = plan.block, plan.slice
    for piece, at in zip(pieces, decode(plan, place, core, pieces)):
        for k in range(plan.tiles // 4):
            matrix = piece[2 * k * half : (2 * k + 2) * half, :]
            tiles = [at(4 * k + n) for n in range(4)]
            vectors = [(right if n % 2 else left)[col] for n, (row, col) in enumerate(tiles)]
            product = lax.dot_general(jnp.concatenate(vectors, axis=0), matrix, NT, preferred_element_type=F32)
            for n, total in enumerate(totals):
                total[tiles[n][0]] += product[n * width : (n + 1) * width]


def multiply_backward(plan, place, core, pieces, upper_left, upper_right, left, right):
    half, width = plan.block, plan.slice
    for piece, at in zip(pieces, decode(plan, place, core, pieces)):
        for k in range(plan.tiles // 4):
            matrix = piece[2 * k * half : (2 * k + 2) * half, :]
            tiles = [at(4 * k + n) for n in range(4)]
            vectors = [(upper_right if n > 1 else upper_left)[row] for n, (row, col) in enumerate(tiles)]
            product = jnp.dot(jnp.concatenate(vectors, axis=0), matrix, preferred_element_type=F32)
            for n, (row, col) in enumerate(tiles):
                (right if n % 2 else left)[col] += product[n * width : (n + 1) * width]


def put_shares(plan, place, left, right, out):
    for m in range(plan.n_row):
        for u in range(plan.n_col):
            at = (place[0] ^ m) * plan.n_col + u
            out[m][u] = join_halves(left, right, at, plan.block).astype(out[m].dtype)


def clear(refs):
    for ref in refs:
        ref[...] = jnp.zeros_like(ref)


def forward_near_kernel(coupling, plan, place, *refs):
    refs = list(refs)
    pieces, received = views(plan, coupling, take(refs, 1)), take(refs, plan.n_row)
    left, right = take(refs, 2)
    totals = refs
    for m in range(plan.n_row):
        for u in range(plan.n_col):
            at = (place[0] ^ m) * plan.n_col + u
            store_halves(left, right, at, received[m][u].astype(F32), plan.block)
    clear(totals)
    multiply_forward(plan, place, 0, pieces, left, right, totals)


def forward_far_kernel(coupling, plan, place, *refs):
    refs = list(refs)
    last = coupling == plan.levels - 1
    sums, stacks = chip_order(take(refs, plan.chips)), take(refs, 2)
    left, right = take(refs, 2)
    near_totals, keep = take(refs, 4), refs.pop(0)
    out = take(refs, plan.n_row if last else 1)
    totals = take(refs, 4)
    pieces = views(plan, coupling, stacks)
    near, far = pieces[: plan.chips], pieces[plan.chips :]
    clear(totals)
    multiply_forward(plan, place, 1, far, left, right, totals)

    if last:
        upper_left, upper_right, back_left, back_right = refs

    def add(refs, at):
        return sum((ref[at] for ref in refs[1:]), refs[0][at])

    def coupled(u):
        all_totals = near_totals + totals
        low, high = all_totals[0:2] + all_totals[4:6], all_totals[2:4] + all_totals[6:8]
        first = add(low, 2 * u) + pltpu.roll(add(high, 2 * u), plan.block, 1)
        second = add(high, 2 * u + 1) + pltpu.roll(add(low, 2 * u + 1), plan.block, 1)
        return jnp.where(low_lanes(first.shape, plan.block), first, second)

    def write(made):
        for _, u, value in made:
            keep[u] = value
            out[0][u] = value.astype(BF16)

    def write_top(made):
        made = [(u, apply_pair_transposed(inverse, value, plan.block)) for inverse, u, value in made]
        for u, value in made:
            keep[u] = value.astype(BF16)
            store_halves(upper_left, upper_right, u, value, plan.block)

    level_forward(plan, place, coupling + 1, sums, pieces, coupled, write_top if last else write)
    if last:
        clear([back_left, back_right])
        multiply_backward(plan, place, 0, near, upper_left, upper_right, back_left, back_right)
        multiply_backward(plan, place, 1, far, upper_left, upper_right, back_left, back_right)
        put_shares(plan, place, back_left, back_right, out)


def backward_kernel(level, plan, place, *refs):
    refs = list(refs)
    sums, pieces = chip_order(take(refs, plan.chips)), views(plan, level - 1, take(refs, 2))
    shares = take(refs, plan.n_row)
    solved, keep = take(refs, 2)
    out = take(refs, plan.n_row)
    upper_left, upper_right, left, right = refs
    clear([left, right])
    back = add_up(shares)

    def write(u, value):
        keep[u] = value.astype(BF16)
        store_halves(upper_left, upper_right, u, value, plan.block)

    level_backward(plan, place, level, sums, pieces, lambda u: solved[u] - back(u), write)
    for core in range(2):
        here = pieces[core * plan.chips : (core + 1) * plan.chips]
        multiply_backward(plan, place, core, here, upper_left, upper_right, left, right)
    put_shares(plan, place, left, right, out)


def leave_kernel(plan, place, *refs):
    refs = list(refs)
    sums, shares = chip_order(take(refs, plan.chips)), take(refs, plan.n_row)
    solved = refs.pop(0)
    above, out = take(refs, plan.levels - 1), refs
    back = add_up(shares)

    def write(u, value):
        for message in out:
            message[u] = value.astype(BF16)

    level_backward(plan, place, 1, sums, [None] * plan.n_col, lambda u: solved[u] - back(u), write)
    for chip, message in enumerate(out):
        base = (place[1] ^ (2 * chip)) // 2 * 2
        for core in range(2):
            for n, level in enumerate(above):
                message[plan.n_col + core * (plan.levels - 1) + n] = level[base + core]


def on_device(n_row, n_col, factor_tiles, tile_row, tile_col, right_sides, diag_inverse):
    plan = Plan(n_row, n_col, factor_tiles, right_sides)
    levels, chips = plan.levels, plan.chips

    def array(shape, kind=BF16):
        return jax.ShapeDtypeStruct(shape, kind)

    def over_row(value, m):
        return lax.ppermute(value, "row", [(i, i ^ m) for i in range(n_row)])

    def over_col(value, m):
        return lax.ppermute(value, "col", [(i, i ^ m) for i in range(n_col)])

    def gather_row(value):
        return [value] + [over_row(value, m) for m in range(1, n_row)]

    def exchange_row(values):
        return [values[0]] + [over_row(values[m], m) for m in range(n_row - 1, 0, -1)]

    def exchange_chips(values):
        return [values[0]] + [over_col(values[m], 2 * m) for m in range(1, chips)]

    def after(values, *others):
        return lax.optimization_barrier((values, others))[0]

    column = (plan.padded, plan.lanes)
    slices = (n_col, plan.slice, plan.lanes)
    dma = pltpu.SemaphoreType.DMA
    x0, message = call(
        plan, first_kernel, [array(column, F32), array(column)], (right_sides[0:1], diag_inverse[0:1])
    )
    tile_row, tile_col = tile_row.transpose(0, 2, 1), tile_col.transpose(0, 2, 1)
    message, tile_row, tile_col = lax.optimization_barrier((message, tile_row, tile_col))
    received = gather_row(message)
    dense, side_slices, inverse_one, *held = call(
        plan, pack_kernel,
        [array((n_row, plan.own * plan.block, plan.lanes)), array((levels,) + column),
         array((plan.block // plan.slice, plan.slice, plan.lanes))]
        + [array((1, plan.payload_rows(), plan.lanes))] * (levels - 1),
        (tile_row, tile_col, factor_tiles, right_sides, diag_inverse),
        scalars=2,
    )

    def join(held, other):
        shape = (2 * held.shape[0],) + held.shape[1:]
        return call(plan, join_kernel, [array(shape)], [held, other])[0]

    def step(held, coupling):
        bit = held.shape[0] if coupling % 2 else chips // 2 // held.shape[0]
        return held, over_col(held, 2 * bit)

    held = [step(value, s) for s, value in enumerate(after(held, received), 1)]
    keep, keep_extra, send = call(
        plan, near_forward_kernel,
        [array((chips,) + slices, F32), array((chips, plan.extra()) + slices[1:]),
         array((chips, n_col + plan.extra()) + slices[1:])],
        [dense] + received + [side_slices, inverse_one],
        [pltpu.VMEM((n_col,) + column, F32)],
    )
    swapped = over_col(send, 1)
    made = call(
        plan, add_kernel, [array(slices, F32)] + [array((n_col + 2 * plan.extra(),) + slices[1:])] * chips,
        [keep, keep_extra, swapped],
    )
    own, sums = made[0], exchange_chips(made[1:])
    held = [join(*value) for value in after(held, sums)]
    if chips > 2:
        held = [step(value, s) for s, value in enumerate(held, 1)]
    solved, message = call(
        plan, enter_kernel, [array(slices, F32), array(slices)], [own] + chip_order(sums)
    )
    solved = [None, solved]

    halves = array((plan.blocks, plan.slice, plan.lanes))
    total = array((plan.own, plan.slice, plan.lanes), F32)
    totals = [pltpu.VMEM(total.shape, F32)] * 4
    backward = [pltpu.VMEM(total.shape, BF16)] * 2 + [pltpu.VMEM(halves.shape, F32)] * 2
    partial = [array(slices, F32)] + [array(slices)] * (n_row - 1)
    pieces = [None]
    for s in range(1, levels):
        received = gather_row(message)
        if s == 1 and chips > 2:
            received, held = lax.optimization_barrier((received, held))
            held = [join(*value) for value in held]
            while held[0].shape[0] < chips:
                held = [join(*step(value, n)) for n, value in enumerate(held, 1)]
        pieces.append([held[s - 1], over_col(held[s - 1], 1)])
        near = call(
            plan, functools.partial(forward_near_kernel, s), [halves] * 2 + [total] * 4,
            pieces[s][:1] + received,
        )
        last = s == levels - 1
        made = call(
            plan, functools.partial(forward_far_kernel, s),
            [array(slices, BF16 if last else F32)] + (partial if last else [array(slices)]),
            chip_order(sums) + pieces[s] + list(near),
            totals + (backward if last else []),
        )
        if not last:
            solved.append(made[0])
            message = made[1]
    results = [made[0]]
    shares = exchange_row(made[1:])
    for level in range(levels - 1, 1, -1):
        made = call(
            plan, functools.partial(backward_kernel, level), [array(slices)] + partial,
            chip_order(sums) + pieces[level - 1] + shares + [solved[level]],
            backward,
        )
        results.insert(0, made[0])
        shares = exchange_row(made[1:])
    messages = call(
        plan, leave_kernel, [array((n_col + 2 * (levels - 1),) + slices[1:])] * chips,
        chip_order(sums) + shares + [solved[1]] + results,
    )
    messages = exchange_chips(messages)
    messages = messages + [over_col(value, 1) for value in messages]
    shares = call(
        plan, near_backward_kernel, [array(column, F32)] + [array(column)] * (n_row - 1), [dense] + messages,
        [pltpu.VMEM((plan.padded, n_col * plan.lanes), BF16)],
    )
    shares = exchange_row(shares)
    result = array(right_sides.shape, F32)
    upper = call(
        plan, upper_out_kernel, [result], messages,
        [pltpu.VMEM((levels,) + column, BF16), pltpu.VMEM((levels,) + right_sides.shape[1:], F32), dma(())],
        raw_out=True,
    )[0]
    args = [diag_inverse, x0] + shares + [upper]
    return call(
        plan, last_kernel, [result], args, [pltpu.VMEM(right_sides.shape[1:], F32), dma(())],
        raw=(len(args) - 1,), raw_out=True, aliases={len(args) - 1: 0},
    )[0]


def solution(mesh):
    return jax.shard_map(
        functools.partial(on_device, mesh.shape["row"], mesh.shape["col"]),
        mesh=mesh,
        in_specs=(
            P(None, "row", None, "col"),
            P(None, "row", "col"),
            P(None, "row", "col"),
            P(None, ("col", "row"), None, None),
            P(None, None, ("col", "row")),
        ),
        out_specs=P(None, ("col", "row"), None, None),
        check_vma=False,
    )
```

```python
import functools

import jax
import jax.numpy as jnp
from jax import lax
from jax.experimental import pallas as pl
from jax.experimental.pallas import tpu as pltpu
from jax.sharding import PartitionSpec as P

BF16 = jnp.bfloat16
F32 = jnp.float32
NT = (((1,), (1,)), ((), ()))
TN = (((0,), (0,)), ((), ()))
SLICE_ROWS = 16


class Plan:
    def __init__(self, n_row, n_col, factor_tiles, right_sides):
        self.levels, self.tiles, self.block, _ = factor_tiles.shape
        self.rows_dev = right_sides.shape[1]
        self.vectors = right_sides.shape[3]
        self.n_row, self.n_col, self.chips = n_row, n_col, n_col // 2
        self.real = self.vectors // n_col
        self.slice = max(SLICE_ROWS, self.real)
        self.padded = self.slice * n_col
        self.lanes = self.rows_dev * self.block
        self.own = n_col * self.rows_dev
        self.blocks = n_row * self.own
        self.tile_rows = self.tiles // 2 * self.block
        self.inverse_at = self.tile_rows + 16
        self.vmem_bytes = (24 if n_col <= 8 else 48) << 20

    def payload_rows(self):
        return self.inverse_at + self.block

    def extra(self):
        return self.levels + self.block // self.slice

    def sources(self):
        return [2 * chip + core for core in range(2) for chip in range(self.chips)]


def call(plan, body, outs, args, scratch=(), scalars=0, raw=(), raw_out=False, aliases=None):
    def kernel(*refs):
        body(plan, (lax.axis_index("row"), lax.axis_index("col")), *refs)

    specs = [pl.BlockSpec(memory_space=pltpu.SMEM)] * scalars
    specs += [pl.BlockSpec(memory_space=pltpu.HBM if n in raw else pltpu.VMEM) for n in range(scalars, len(args))]
    return pl.pallas_call(
        kernel,
        out_shape=outs,
        in_specs=specs,
        out_specs=[pl.BlockSpec(memory_space=pltpu.HBM if raw_out else pltpu.VMEM)] * len(outs),
        scratch_shapes=list(scratch),
        input_output_aliases=aliases or {},
        compiler_params=pltpu.CompilerParams(vmem_limit_bytes=plan.vmem_bytes),
    )(*args)


def chip_order(values):
    return [values[0], *values[:0:-1]]


def take(refs, count):
    return [refs.pop(0) for _ in range(count)]


def low_lanes(shape, half):
    return lax.broadcasted_iota(jnp.int32, shape, len(shape) - 1) < half


def split_rows(value):
    high = value.astype(BF16)
    return jnp.concatenate([high, (value - high.astype(F32)).astype(BF16)], axis=0)


def apply_pair(inverse, value, half):
    n = value.shape[0]
    both = jnp.concatenate([value, pltpu.roll(value, half, 1)], axis=0)[:, :half]
    out = jnp.dot(split_rows(both), inverse, preferred_element_type=F32)
    out = out[: 2 * n] + out[2 * n :]
    return jnp.where(low_lanes((n, 2 * half), half), out[:n], out[n:])


def apply_pair_transposed(inverse, value, half):
    n = value.shape[0]
    low = low_lanes(value.shape, half)
    both = jnp.concatenate([jnp.where(low, value, 0.0), jnp.where(low, 0.0, value)], axis=0)
    out = lax.dot_general(split_rows(both), inverse, NT, preferred_element_type=F32)
    out = out[: 2 * n] + out[2 * n :]
    return jnp.concatenate([out[:n], out[n:]], axis=1)


def pad_slices(plan, value, out):
    if plan.real == plan.slice:
        out[...] = value.astype(out.dtype)
        return
    out[...] = jnp.zeros_like(out)
    for c in range(plan.n_col):
        out[c * plan.slice : c * plan.slice + plan.real, :] = value[c * plan.real : (c + 1) * plan.real].astype(out.dtype)


def drop_padding(plan, value):
    if plan.real == plan.slice:
        return value
    return jnp.concatenate([value[c * plan.slice : c * plan.slice + plan.real] for c in range(plan.n_col)], axis=0)


def store_halves(left, right, at, value, half):
    low = low_lanes(value.shape, half)
    other = pltpu.roll(value, half, 1)
    left[2 * at] = jnp.where(low, value, 0.0).astype(BF16)
    right[2 * at] = jnp.where(low, 0.0, other).astype(BF16)
    left[2 * at + 1] = jnp.where(low, other, 0.0).astype(BF16)
    right[2 * at + 1] = jnp.where(low, 0.0, value).astype(BF16)


def join_halves(left, right, at, half):
    first = left[2 * at] + pltpu.roll(right[2 * at], half, 1)
    second = right[2 * at + 1] + pltpu.roll(left[2 * at + 1], half, 1)
    return jnp.where(low_lanes(first.shape, half), first, second)


def pack_kernel(plan, place, rows, cols, *refs):
    refs = list(refs)
    tiles, sides, inverse = take(refs, 3)
    dense, side_slices, inverse_one = take(refs, 3)
    payloads = take(refs, plan.levels - 1)
    half = plan.block
    lane = lax.broadcasted_iota(jnp.int32, (16, 128), 1)
    for coupling in range(plan.levels):
        if coupling == 0:
            dense[...] = jnp.zeros_like(dense)
            for t in range(plan.tiles):
                tile = tiles[0, t]
                col = cols[0, 0, t]
                both = jnp.concatenate([tile, tile], axis=1).astype(F32)
                here = (lax.broadcasted_iota(jnp.int32, both.shape, 1) // half) == col % 2
                at = pl.ds(pl.multiple_of(rows[0, 0, t] * half, half), half)
                dense[col // 2, at, :] += jnp.where(here, both, 0.0).astype(BF16)
            continue
        target = payloads[coupling - 1].at[0]
        for k in range(plan.tiles // 2):
            pair = jnp.concatenate([tiles[coupling, 2 * k], tiles[coupling, 2 * k + 1]], axis=1)
            target[k * half : (k + 1) * half, :] = pair
        index = jnp.zeros((16, 128), F32)
        for t in range(plan.tiles):
            index = jnp.where(lane == t, rows[coupling, 0, t].astype(F32), index)
            index = jnp.where(lane == t + 64, cols[coupling, 0, t].astype(F32), index)
        target[plan.tile_rows : plan.inverse_at, :] = index.astype(BF16)
    inverse_one[...] = inverse[1].astype(BF16).reshape(inverse_one.shape)
    for level in range(1, plan.levels + 1):
        if level > 1:
            payloads[level - 2][0, plan.inverse_at :, :] = inverse[level].astype(BF16)
        both = jnp.concatenate([sides[level, b] for b in range(plan.rows_dev)], axis=0).T
        pad_slices(plan, both, side_slices.at[level - 1])


def near_forward_kernel(plan, place, dense, *refs):
    refs = list(refs)
    received = take(refs, plan.n_row)
    side_slices, inverse_one = take(refs, 2)
    keep, keep_extra, send, total = refs
    width, lanes = plan.slice, plan.lanes
    vectors = jnp.concatenate([ref[...] for ref in received], axis=1)
    for u in range(0, plan.n_col, 2):
        matrix = [dense[place[0] ^ m, u * lanes : (u + 2) * lanes, :] for m in range(plan.n_row)]
        matrix = jnp.concatenate(matrix, axis=1)
        product = lax.dot_general(vectors, matrix, NT, preferred_element_type=F32)
        for n in range(2):
            total[u + n] = product[:, n * lanes : (n + 1) * lanes]
    for chip in range(plan.chips):
        for core, (out, extra, at) in enumerate(((keep, keep_extra, 0), (send, send, plan.n_col))):
            number = place[1] ^ (2 * chip + core)
            here = pl.ds(pl.multiple_of(number * width, 16), width)
            for u in range(plan.n_col):
                out[chip, u] = total[u, here, :].astype(out.dtype)
            for level in range(plan.levels):
                extra[chip, at + level] = side_slices[level, here, :]
            extra[chip, at + plan.levels : at + plan.extra()] = inverse_one[...]


def add_kernel(plan, place, keep, keep_extra, received, own, *out):
    here = plan.n_col + (place[1] & 1) * plan.extra()
    there = plan.n_col + (1 - (place[1] & 1)) * plan.extra()
    own[...] = keep[0] + received[0, : plan.n_col].astype(F32)
    for chip in range(plan.chips):
        if chip:
            total = keep[chip] + received[chip, : plan.n_col].astype(F32)
            out[chip][: plan.n_col] = total.astype(BF16)
        out[chip][pl.ds(here, plan.extra())] = keep_extra[chip]
        out[chip][pl.ds(there, plan.extra())] = received[chip, plan.n_col :]


def near_backward_kernel(plan, place, dense, *refs):
    refs = list(refs)
    received = take(refs, plan.n_col)
    out = take(refs, plan.n_row)
    (upper,) = refs
    width, lanes = plan.slice, plan.lanes
    for piece, offset in zip(received, plan.sources()):
        here = pl.ds(pl.multiple_of((place[1] ^ offset) * width, 16), width)
        for u in range(plan.n_col):
            upper[here, u * lanes : (u + 1) * lanes] = piece[u]
    vectors = upper[...]
    for m in range(0, plan.n_row, 2):
        matrix = jnp.concatenate([dense[place[0] ^ m], dense[place[0] ^ (m + 1)]], axis=1)
        product = jnp.dot(vectors, matrix, preferred_element_type=F32)
        for n in range(2):
            out[m + n][...] = product[:, n * lanes : (n + 1) * lanes].astype(out[m + n].dtype)


def upper_out_kernel(plan, place, *refs):
    refs = list(refs)
    pieces = take(refs, plan.n_col)
    out, all_slices, result, sem = refs
    half, width = plan.block, plan.slice
    core = place[1] & 1
    for piece, offset in zip(pieces, plan.sources()):
        here = pl.ds(pl.multiple_of((place[1] ^ offset) * width, 16), width)
        all_slices[0, here, :] = piece[place[1]]
        for n in range(1, plan.levels):
            all_slices[n, here, :] = piece[plan.n_col + core * (plan.levels - 1) + n - 1]
    for n in range(plan.levels):
        value = drop_padding(plan, all_slices[n].astype(F32)).T
        for b in range(plan.rows_dev):
            result[n, b] = value[b * half : (b + 1) * half, :]
    copy = pltpu.make_async_copy(result, out.at[1:], sem)
    copy.start()
    copy.wait()


def last_kernel(plan, place, inverse, solved, *refs):
    refs = list(refs)
    shares = take(refs, plan.n_row)
    _, out, result, sem = refs
    half = plan.block
    back = shares[0][...].astype(F32)
    for share in shares[1:]:
        back = back + share[...].astype(F32)
    value = drop_padding(plan, solved[...] - back)
    for b in range(plan.rows_dev):
        cut = slice(b * half, (b + 1) * half)
        result[b] = lax.dot_general(inverse[0, :, cut], value[:, cut], NT,
                                    precision=lax.Precision.HIGHEST, preferred_element_type=F32)
    copy = pltpu.make_async_copy(result, out.at[0], sem)
    copy.start()
    copy.wait()


def extras(plan, place, sums):
    core = place[1] & 1
    return [(sums[chip], plan.n_col + (core ^ other) * plan.extra()) for other in range(2) for chip in range(plan.chips)]


def inverse_of(plan, level, extra, piece):
    if level == 1:
        ref, at = extra
        return ref[pl.ds(at + plan.levels, plan.block // plan.slice)].reshape(plan.block, plan.lanes)
    return piece[plan.inverse_at :, :]


def level_forward(plan, place, level, sums, pieces, coupled, write):
    made = []
    for extra, piece, offset in zip(extras(plan, place, sums), pieces, plan.sources()):
        u = place[1] ^ offset
        side = extra[0][extra[1] + level - 1].astype(F32)
        inverse = inverse_of(plan, level, extra, piece)
        made.append((inverse, u, apply_pair(inverse, side - coupled(u), plan.block)))
    write(made)


def level_backward(plan, place, level, sums, pieces, value, write):
    made = []
    for extra, piece, offset in zip(extras(plan, place, sums), pieces, plan.sources()):
        u = place[1] ^ offset
        made.append((u, apply_pair_transposed(inverse_of(plan, level, extra, piece), value(u), plan.block)))
    for u, value in made:
        write(u, value)


def join_kernel(plan, place, first, second, out):
    count = first.shape[0]
    out[:count] = first[...]
    out[count:] = second[...]


def views(plan, coupling, refs):
    order = list(range(plan.chips))
    if coupling % 2 == 0:
        bits = plan.chips.bit_length() - 1
        order = [sum(((chip >> n) & 1) << (bits - 1 - n) for n in range(bits)) for chip in order]
    return [ref.at[chip] for ref in refs for chip in order]


def add_up(refs):
    def total(u):
        value = refs[0][u].astype(F32)
        for ref in refs[1:]:
            value = value + ref[u].astype(F32)
        return value

    return total


def enter_kernel(plan, place, *refs):
    refs = list(refs)
    own, sums = refs.pop(0), chip_order(take(refs, plan.chips))
    solved, message = refs

    def write(made):
        for _, u, value in made:
            solved[u] = value
            message[u] = value.astype(BF16)

    coupled = add_up([own] + sums[1:])
    level_forward(plan, place, 1, sums, [None] * plan.n_col, coupled, write)


def decode(plan, place, core, pieces):
    def reader(row, col):
        return lambda tile: (row[0, tile], col[0, tile + 64])

    readers = []
    for chip, piece in enumerate(pieces):
        raw = piece[plan.tile_rows : plan.inverse_at, :].astype(F32).astype(jnp.int32)[0:1]
        owner = raw // plan.rows_dev * plan.n_col + (place[1] ^ (2 * chip + core))
        readers.append(reader(raw, owner * plan.rows_dev + raw % plan.rows_dev))
    return readers


def multiply_forward(plan, place, core, pieces, left, right, totals):
    half, width = plan.block, plan.slice
    for piece, at in zip(pieces, decode(plan, place, core, pieces)):
        for k in range(plan.tiles // 4):
            matrix = piece[2 * k * half : (2 * k + 2) * half, :]
            tiles = [at(4 * k + n) for n in range(4)]
            vectors = [(right if n % 2 else left)[col] for n, (row, col) in enumerate(tiles)]
            product = lax.dot_general(jnp.concatenate(vectors, axis=0), matrix, NT, preferred_element_type=F32)
            for n, total in enumerate(totals):
                total[tiles[n][0]] += product[n * width : (n + 1) * width]


def multiply_backward(plan, place, core, pieces, upper_left, upper_right, left, right):
    half, width = plan.block, plan.slice
    for piece, at in zip(pieces, decode(plan, place, core, pieces)):
        for k in range(plan.tiles // 4):
            matrix = piece[2 * k * half : (2 * k + 2) * half, :]
            tiles = [at(4 * k + n) for n in range(4)]
            vectors = [(upper_right if n > 1 else upper_left)[row] for n, (row, col) in enumerate(tiles)]
            product = jnp.dot(jnp.concatenate(vectors, axis=0), matrix, preferred_element_type=F32)
            for n, (row, col) in enumerate(tiles):
                (right if n % 2 else left)[col] += product[n * width : (n + 1) * width]


def put_shares(plan, place, left, right, out):
    for m in range(plan.n_row):
        for u in range(plan.n_col):
            at = (place[0] ^ m) * plan.n_col + u
            out[m][u] = join_halves(left, right, at, plan.block).astype(out[m].dtype)


def clear(refs):
    for ref in refs:
        ref[...] = jnp.zeros_like(ref)


def forward_near_kernel(coupling, plan, place, *refs):
    refs = list(refs)
    pieces, received = views(plan, coupling, take(refs, 1)), take(refs, plan.n_row)
    left, right = take(refs, 2)
    totals = refs
    for m in range(plan.n_row):
        for u in range(plan.n_col):
            at = (place[0] ^ m) * plan.n_col + u
            store_halves(left, right, at, received[m][u].astype(F32), plan.block)
    clear(totals)
    multiply_forward(plan, place, 0, pieces, left, right, totals)


def forward_far_kernel(coupling, plan, place, *refs):
    refs = list(refs)
    last = coupling == plan.levels - 1
    sums, stacks = chip_order(take(refs, plan.chips)), take(refs, 2)
    left, right = take(refs, 2)
    near_totals, keep = take(refs, 4), refs.pop(0)
    out = take(refs, plan.n_row if last else 1)
    totals = take(refs, 4)
    pieces = views(plan, coupling, stacks)
    near, far = pieces[: plan.chips], pieces[plan.chips :]
    clear(totals)
    multiply_forward(plan, place, 1, far, left, right, totals)

    if last:
        upper_left, upper_right, back_left, back_right = refs

    def add(refs, at):
        return sum((ref[at] for ref in refs[1:]), refs[0][at])

    def coupled(u):
        all_totals = near_totals + totals
        low, high = all_totals[0:2] + all_totals[4:6], all_totals[2:4] + all_totals[6:8]
        first = add(low, 2 * u) + pltpu.roll(add(high, 2 * u), plan.block, 1)
        second = add(high, 2 * u + 1) + pltpu.roll(add(low, 2 * u + 1), plan.block, 1)
        return jnp.where(low_lanes(first.shape, plan.block), first, second)

    def write(made):
        for _, u, value in made:
            keep[u] = value
            out[0][u] = value.astype(BF16)

    def write_top(made):
        made = [(u, apply_pair_transposed(inverse, value, plan.block)) for inverse, u, value in made]
        for u, value in made:
            keep[u] = value.astype(BF16)
            store_halves(upper_left, upper_right, u, value, plan.block)

    level_forward(plan, place, coupling + 1, sums, pieces, coupled, write_top if last else write)
    if last:
        clear([back_left, back_right])
        multiply_backward(plan, place, 0, near, upper_left, upper_right, back_left, back_right)
        multiply_backward(plan, place, 1, far, upper_left, upper_right, back_left, back_right)
        put_shares(plan, place, back_left, back_right, out)


def backward_kernel(level, plan, place, *refs):
    refs = list(refs)
    sums, pieces = chip_order(take(refs, plan.chips)), views(plan, level - 1, take(refs, 2))
    shares = take(refs, plan.n_row)
    solved, keep = take(refs, 2)
    out = take(refs, plan.n_row)
    upper_left, upper_right, left, right = refs
    clear([left, right])
    back = add_up(shares)

    def write(u, value):
        keep[u] = value.astype(BF16)
        store_halves(upper_left, upper_right, u, value, plan.block)

    level_backward(plan, place, level, sums, pieces, lambda u: solved[u] - back(u), write)
    for core in range(2):
        here = pieces[core * plan.chips : (core + 1) * plan.chips]
        multiply_backward(plan, place, core, here, upper_left, upper_right, left, right)
    put_shares(plan, place, left, right, out)


def leave_kernel(plan, place, *refs):
    refs = list(refs)
    sums, shares = chip_order(take(refs, plan.chips)), take(refs, plan.n_row)
    solved = refs.pop(0)
    above, out = take(refs, plan.levels - 1), refs
    back = add_up(shares)

    def write(u, value):
        for message in out:
            message[u] = value.astype(BF16)

    level_backward(plan, place, 1, sums, [None] * plan.n_col, lambda u: solved[u] - back(u), write)
    for chip, message in enumerate(out):
        base = (place[1] ^ (2 * chip)) // 2 * 2
        for core in range(2):
            for n, level in enumerate(above):
                message[plan.n_col + core * (plan.levels - 1) + n] = level[base + core]


def on_device(n_row, n_col, factor_tiles, tile_row, tile_col, right_sides, diag_inverse):
    plan = Plan(n_row, n_col, factor_tiles, right_sides)
    levels, chips = plan.levels, plan.chips

    def array(shape, kind=BF16):
        return jax.ShapeDtypeStruct(shape, kind)

    def over_row(value, m):
        return lax.ppermute(value, "row", [(i, i ^ m) for i in range(n_row)])

    def over_col(value, m):
        return lax.ppermute(value, "col", [(i, i ^ m) for i in range(n_col)])

    def gather_row(value):
        return [value] + [over_row(value, m) for m in range(1, n_row)]

    def exchange_row(values):
        return [values[0]] + [over_row(values[m], m) for m in range(n_row - 1, 0, -1)]

    def exchange_chips(values):
        return [values[0]] + [over_col(values[m], 2 * m) for m in range(1, chips)]

    def after(values, *others):
        return lax.optimization_barrier((values, others))[0]

    column = (plan.padded, plan.lanes)
    slices = (n_col, plan.slice, plan.lanes)
    dma = pltpu.SemaphoreType.DMA
    x0 = lax.dot_general(right_sides[0], diag_inverse[0], (((1,), (0,)), ((), ())), precision=lax.Precision.HIGHEST)
    owner = jnp.arange(plan.lanes) // plan.block
    x0 = sum(jnp.where(owner == b, x0[b], 0.0) for b in range(plan.rows_dev))
    x0 = x0.reshape(n_col, plan.real, plan.lanes)
    x0 = jnp.pad(x0, ((0, 0), (0, plan.slice - plan.real), (0, 0))).reshape(column)
    message = x0.astype(BF16)
    tile_row, tile_col = tile_row.transpose(0, 2, 1), tile_col.transpose(0, 2, 1)
    message, tile_row, tile_col = lax.optimization_barrier((message, tile_row, tile_col))
    received = gather_row(message)
    dense, side_slices, inverse_one, *held = call(
        plan, pack_kernel,
        [array((n_row, plan.own * plan.block, plan.lanes)), array((levels,) + column),
         array((plan.block // plan.slice, plan.slice, plan.lanes))]
        + [array((1, plan.payload_rows(), plan.lanes))] * (levels - 1),
        (tile_row, tile_col, factor_tiles, right_sides, diag_inverse),
        scalars=2,
    )

    def join(held, other):
        shape = (2 * held.shape[0],) + held.shape[1:]
        return call(plan, join_kernel, [array(shape)], [held, other])[0]

    def step(held, coupling):
        bit = held.shape[0] if coupling % 2 else chips // 2 // held.shape[0]
        return held, over_col(held, 2 * bit)

    held = [step(value, s) for s, value in enumerate(after(held, received), 1)]
    keep, keep_extra, send = call(
        plan, near_forward_kernel,
        [array((chips,) + slices, F32), array((chips, plan.extra()) + slices[1:]),
         array((chips, n_col + plan.extra()) + slices[1:])],
        [dense] + received + [side_slices, inverse_one],
        [pltpu.VMEM((n_col,) + column, F32)],
    )
    swapped = over_col(send, 1)
    made = call(
        plan, add_kernel, [array(slices, F32)] + [array((n_col + 2 * plan.extra(),) + slices[1:])] * chips,
        [keep, keep_extra, swapped],
    )
    own, sums = made[0], exchange_chips(made[1:])
    held = [join(*value) for value in after(held, sums)]
    if chips > 2:
        held = [step(value, s) for s, value in enumerate(held, 1)]
    solved, message = call(
        plan, enter_kernel, [array(slices, F32), array(slices)], [own] + chip_order(sums)
    )
    solved = [None, solved]

    halves = array((plan.blocks, plan.slice, plan.lanes))
    total = array((plan.own, plan.slice, plan.lanes), F32)
    totals = [pltpu.VMEM(total.shape, F32)] * 4
    backward = [pltpu.VMEM(total.shape, BF16)] * 2 + [pltpu.VMEM(halves.shape, F32)] * 2
    partial = [array(slices, F32)] + [array(slices)] * (n_row - 1)
    pieces = [None]
    for s in range(1, levels):
        received = gather_row(message)
        if s == 1 and chips > 2:
            received, held = lax.optimization_barrier((received, held))
            held = [join(*value) for value in held]
            while held[0].shape[0] < chips:
                held = [join(*step(value, n)) for n, value in enumerate(held, 1)]
        pieces.append([held[s - 1], over_col(held[s - 1], 1)])
        near = call(
            plan, functools.partial(forward_near_kernel, s), [halves] * 2 + [total] * 4,
            pieces[s][:1] + received,
        )
        last = s == levels - 1
        made = call(
            plan, functools.partial(forward_far_kernel, s),
            [array(slices, BF16 if last else F32)] + (partial if last else [array(slices)]),
            chip_order(sums) + pieces[s] + list(near),
            totals + (backward if last else []),
        )
        if not last:
            solved.append(made[0])
            message = made[1]
    results = [made[0]]
    shares = exchange_row(made[1:])
    for level in range(levels - 1, 1, -1):
        made = call(
            plan, functools.partial(backward_kernel, level), [array(slices)] + partial,
            chip_order(sums) + pieces[level - 1] + shares + [solved[level]],
            backward,
        )
        results.insert(0, made[0])
        shares = exchange_row(made[1:])
    messages = call(
        plan, leave_kernel, [array((n_col + 2 * (levels - 1),) + slices[1:])] * chips,
        chip_order(sums) + shares + [solved[1]] + results,
    )
    messages = exchange_chips(messages)
    messages = messages + [over_col(value, 1) for value in messages]
    shares = call(
        plan, near_backward_kernel, [array(column, F32)] + [array(column)] * (n_row - 1), [dense] + messages,
        [pltpu.VMEM((plan.padded, n_col * plan.lanes), BF16)],
    )
    shares = exchange_row(shares)
    result = array(right_sides.shape, F32)
    upper = call(
        plan, upper_out_kernel, [result], messages,
        [pltpu.VMEM((levels,) + column, BF16), pltpu.VMEM((levels,) + right_sides.shape[1:], F32), dma(())],
        raw_out=True,
    )[0]
    args = [diag_inverse, x0] + shares + [upper]
    return call(
        plan, last_kernel, [result], args, [pltpu.VMEM(right_sides.shape[1:], F32), dma(())],
        raw=(len(args) - 1,), raw_out=True, aliases={len(args) - 1: 0},
    )[0]


def solution(mesh):
    return jax.shard_map(
        functools.partial(on_device, mesh.shape["row"], mesh.shape["col"]),
        mesh=mesh,
        in_specs=(
            P(None, "row", None, "col"),
            P(None, "row", "col"),
            P(None, "row", "col"),
            P(None, ("col", "row"), None, None),
            P(None, None, ("col", "row")),
        ),
        out_specs=P(None, ("col", "row"), None, None),
        check_vma=False,
    )
```

```python
import functools

import jax
import jax.numpy as jnp
from jax import lax
from jax.experimental import pallas as pl
from jax.experimental.pallas import tpu as pltpu
from jax.sharding import PartitionSpec as P

BF16 = jnp.bfloat16
F32 = jnp.float32
NT = (((1,), (1,)), ((), ()))
TN = (((0,), (0,)), ((), ()))
SLICE_ROWS = 16


class Plan:
    def __init__(self, n_row, n_col, factor_tiles, right_sides):
        self.levels, self.tiles, self.block, _ = factor_tiles.shape
        self.rows_dev = right_sides.shape[1]
        self.vectors = right_sides.shape[3]
        self.n_row, self.n_col, self.chips = n_row, n_col, n_col // 2
        self.real = self.vectors // n_col
        self.slice = max(SLICE_ROWS, self.real)
        self.padded = self.slice * n_col
        self.lanes = self.rows_dev * self.block
        self.own = n_col * self.rows_dev
        self.blocks = n_row * self.own
        self.tile_rows = self.tiles // 2 * self.block
        self.inverse_at = self.tile_rows + 16
        self.vmem_bytes = (24 if n_col <= 8 else 48) << 20

    def payload_rows(self):
        return self.inverse_at + self.block

    def extra(self):
        return self.levels - 1 + self.block // self.slice

    def sources(self):
        return [2 * chip + core for core in range(2) for chip in range(self.chips)]


def call(plan, body, outs, args, scratch=(), scalars=0, raw=(), raw_out=False, aliases=None):
    def kernel(*refs):
        body(plan, (lax.axis_index("row"), lax.axis_index("col")), *refs)

    specs = [pl.BlockSpec(memory_space=pltpu.SMEM)] * scalars
    specs += [pl.BlockSpec(memory_space=pltpu.HBM if n in raw else pltpu.VMEM) for n in range(scalars, len(args))]
    return pl.pallas_call(
        kernel,
        out_shape=outs,
        in_specs=specs,
        out_specs=[pl.BlockSpec(memory_space=pltpu.HBM if raw_out else pltpu.VMEM)] * len(outs),
        scratch_shapes=list(scratch),
        input_output_aliases=aliases or {},
        compiler_params=pltpu.CompilerParams(vmem_limit_bytes=plan.vmem_bytes),
    )(*args)


def chip_order(values):
    return [values[0], *values[:0:-1]]


def take(refs, count):
    return [refs.pop(0) for _ in range(count)]


def low_lanes(shape, half):
    return lax.broadcasted_iota(jnp.int32, shape, len(shape) - 1) < half


def split_rows(value):
    high = value.astype(BF16)
    return jnp.concatenate([high, (value - high.astype(F32)).astype(BF16)], axis=0)


def apply_pair(inverse, value, half):
    n = value.shape[0]
    both = jnp.concatenate([value, pltpu.roll(value, half, 1)], axis=0)[:, :half]
    out = jnp.dot(split_rows(both), inverse, preferred_element_type=F32)
    out = out[: 2 * n] + out[2 * n :]
    return jnp.where(low_lanes((n, 2 * half), half), out[:n], out[n:])


def apply_pair_transposed(inverse, value, half):
    n = value.shape[0]
    low = low_lanes(value.shape, half)
    both = jnp.concatenate([jnp.where(low, value, 0.0), jnp.where(low, 0.0, value)], axis=0)
    out = lax.dot_general(split_rows(both), inverse, NT, preferred_element_type=F32)
    out = out[: 2 * n] + out[2 * n :]
    return jnp.concatenate([out[:n], out[n:]], axis=1)


def pad_slices(plan, value, out):
    if plan.real == plan.slice:
        out[...] = value.astype(out.dtype)
        return
    out[...] = jnp.zeros_like(out)
    for c in range(plan.n_col):
        out[c * plan.slice : c * plan.slice + plan.real, :] = value[c * plan.real : (c + 1) * plan.real].astype(out.dtype)


def drop_padding(plan, value):
    if plan.real == plan.slice:
        return value
    return jnp.concatenate([value[c * plan.slice : c * plan.slice + plan.real] for c in range(plan.n_col)], axis=0)


def store_halves(left, right, at, value, half):
    low = low_lanes(value.shape, half)
    other = pltpu.roll(value, half, 1)
    left[2 * at] = jnp.where(low, value, 0.0).astype(BF16)
    right[2 * at] = jnp.where(low, 0.0, other).astype(BF16)
    left[2 * at + 1] = jnp.where(low, other, 0.0).astype(BF16)
    right[2 * at + 1] = jnp.where(low, 0.0, value).astype(BF16)


def join_halves(left, right, at, half):
    first = left[2 * at] + pltpu.roll(right[2 * at], half, 1)
    second = right[2 * at + 1] + pltpu.roll(left[2 * at + 1], half, 1)
    return jnp.where(low_lanes(first.shape, half), first, second)


def pack_kernel(plan, place, rows, cols, *refs):
    refs = list(refs)
    tiles, sides, inverse = take(refs, 3)
    dense, side_slices, inverse_one = take(refs, 3)
    payloads = take(refs, plan.levels - 1)
    half = plan.block
    lane = lax.broadcasted_iota(jnp.int32, (16, 128), 1)
    for coupling in range(plan.levels):
        if coupling == 0:
            dense[...] = jnp.zeros_like(dense)
            for t in range(plan.tiles):
                tile = tiles[0, t]
                col = cols[0, 0, t]
                both = jnp.concatenate([tile, tile], axis=1).astype(F32)
                here = (lax.broadcasted_iota(jnp.int32, both.shape, 1) // half) == col % 2
                at = pl.ds(pl.multiple_of(rows[0, 0, t] * half, half), half)
                dense[col // 2, at, :] += jnp.where(here, both, 0.0).astype(BF16)
            continue
        target = payloads[coupling - 1].at[0]
        for k in range(plan.tiles // 2):
            pair = jnp.concatenate([tiles[coupling, 2 * k], tiles[coupling, 2 * k + 1]], axis=1)
            target[k * half : (k + 1) * half, :] = pair
        index = jnp.zeros((16, 128), F32)
        for t in range(plan.tiles):
            index = jnp.where(lane == t, rows[coupling, 0, t].astype(F32), index)
            index = jnp.where(lane == t + 64, cols[coupling, 0, t].astype(F32), index)
        target[plan.tile_rows : plan.inverse_at, :] = index.astype(BF16)
    inverse_one[...] = inverse[1].astype(BF16).reshape(inverse_one.shape)
    for level in range(1, plan.levels + 1):
        if level > 1:
            payloads[level - 2][0, plan.inverse_at :, :] = inverse[level].astype(BF16)
        both = jnp.concatenate([sides[level, b] for b in range(plan.rows_dev)], axis=0).T
        pad_slices(plan, both, side_slices.at[level - 1])


def near_forward_kernel(plan, place, dense, *refs):
    refs = list(refs)
    received = take(refs, plan.n_row)
    side_slices, inverse_one = take(refs, 2)
    keep, keep_extra, send, total = refs
    width, lanes = plan.slice, plan.lanes
    vectors = jnp.concatenate([ref[...] for ref in received], axis=1)
    for u in range(0, plan.n_col, 2):
        matrix = [dense[place[0] ^ m, u * lanes : (u + 2) * lanes, :] for m in range(plan.n_row)]
        matrix = jnp.concatenate(matrix, axis=1)
        product = lax.dot_general(vectors, matrix, NT, preferred_element_type=F32)
        for n in range(2):
            total[u + n] = product[:, n * lanes : (n + 1) * lanes]
    for chip in range(plan.chips):
        for core, (out, extra, at) in enumerate(((keep, keep_extra, 0), (send, send, plan.n_col))):
            number = place[1] ^ (2 * chip + core)
            here = pl.ds(pl.multiple_of(number * width, 16), width)
            for u in range(plan.n_col):
                out[chip, u] = total[u, here, :].astype(out.dtype)
            mine = total[place[1], here, :] - side_slices[0, here, :].astype(F32)
            out[chip, place[1]] = mine.astype(out.dtype)
            for level in range(1, plan.levels):
                extra[chip, at + level - 1] = side_slices[level, here, :]
            extra[chip, at + plan.levels - 1 : at + plan.extra()] = inverse_one[...]


def add_kernel(plan, place, keep, keep_extra, received, own, *out):
    here = plan.n_col + (place[1] & 1) * plan.extra()
    there = plan.n_col + (1 - (place[1] & 1)) * plan.extra()
    own[...] = keep[0] + received[0, : plan.n_col].astype(F32)
    for chip in range(plan.chips):
        if chip:
            total = keep[chip] + received[chip, : plan.n_col].astype(F32)
            out[chip][: plan.n_col] = total.astype(BF16)
        out[chip][pl.ds(here, plan.extra())] = keep_extra[chip]
        out[chip][pl.ds(there, plan.extra())] = received[chip, plan.n_col :]


def near_backward_kernel(plan, place, dense, *refs):
    refs = list(refs)
    received = chip_order(take(refs, plan.chips)) + chip_order(take(refs, plan.chips))
    out = take(refs, plan.n_row)
    (upper,) = refs
    width, lanes = plan.slice, plan.lanes
    for piece, offset in zip(received, plan.sources()):
        here = pl.ds(pl.multiple_of((place[1] ^ offset) * width, 16), width)
        for u in range(plan.n_col):
            upper[here, u * lanes : (u + 1) * lanes] = piece[u]
    vectors = upper[...]
    for m in range(0, plan.n_row, 2):
        matrix = jnp.concatenate([dense[place[0] ^ m], dense[place[0] ^ (m + 1)]], axis=1)
        product = jnp.dot(vectors, matrix, preferred_element_type=F32)
        for n in range(2):
            out[m + n][...] = product[:, n * lanes : (n + 1) * lanes].astype(out[m + n].dtype)


def upper_out_kernel(plan, place, *refs):
    refs = list(refs)
    pieces = chip_order(take(refs, plan.chips)) + chip_order(take(refs, plan.chips))
    out, all_slices, result, sem = refs
    half, width = plan.block, plan.slice
    core = place[1] & 1
    for piece, offset in zip(pieces, plan.sources()):
        here = pl.ds(pl.multiple_of((place[1] ^ offset) * width, 16), width)
        all_slices[0, here, :] = piece[place[1]]
        for n in range(1, plan.levels):
            all_slices[n, here, :] = piece[plan.n_col + core * (plan.levels - 1) + n - 1]
    for n in range(plan.levels):
        value = drop_padding(plan, all_slices[n].astype(F32)).T
        for b in range(plan.rows_dev):
            result[n, b] = value[b * half : (b + 1) * half, :]
    copy = pltpu.make_async_copy(result, out.at[1:], sem)
    copy.start()
    copy.wait()


def last_kernel(plan, place, inverse, solved, *refs):
    refs = list(refs)
    shares = take(refs, plan.n_row)
    _, out, result, sem = refs
    half = plan.block
    back = shares[0][...].astype(F32)
    for share in shares[1:]:
        back = back + share[...].astype(F32)
    value = drop_padding(plan, solved[...] - back)
    for b in range(plan.rows_dev):
        cut = slice(b * half, (b + 1) * half)
        result[b] = lax.dot_general(inverse[0, :, cut], value[:, cut], NT,
                                    precision=lax.Precision.HIGHEST, preferred_element_type=F32)
    copy = pltpu.make_async_copy(result, out.at[0], sem)
    copy.start()
    copy.wait()


def extras(plan, place, sums):
    core = place[1] & 1
    return [(sums[chip], plan.n_col + (core ^ other) * plan.extra()) for other in range(2) for chip in range(plan.chips)]


def inverse_of(plan, level, extra, piece):
    if level == 1:
        ref, at = extra
        return ref[pl.ds(at + plan.levels - 1, plan.block // plan.slice)].reshape(plan.block, plan.lanes)
    return piece[plan.inverse_at :, :]


def level_forward(plan, place, level, sums, pieces, coupled, write):
    made = []
    for extra, piece, offset in zip(extras(plan, place, sums), pieces, plan.sources()):
        u = place[1] ^ offset
        value = -coupled(u)
        if level > 1:
            value = extra[0][extra[1] + level - 2].astype(F32) + value
        inverse = inverse_of(plan, level, extra, piece)
        made.append((inverse, u, apply_pair(inverse, value, plan.block)))
    write(made)


def level_backward(plan, place, level, sums, pieces, value, write):
    made = []
    for extra, piece, offset in zip(extras(plan, place, sums), pieces, plan.sources()):
        u = place[1] ^ offset
        made.append((u, apply_pair_transposed(inverse_of(plan, level, extra, piece), value(u), plan.block)))
    for u, value in made:
        write(u, value)


def join_kernel(plan, place, first, second, out):
    count = first.shape[0]
    out[:count] = first[...]
    out[count:] = second[...]


def views(plan, coupling, refs):
    order = list(range(plan.chips))
    if coupling % 2 == 0:
        bits = plan.chips.bit_length() - 1
        order = [sum(((chip >> n) & 1) << (bits - 1 - n) for n in range(bits)) for chip in order]
    return [ref.at[chip] for ref in refs for chip in order]


def add_up(refs):
    def total(u):
        value = refs[0][u].astype(F32)
        for ref in refs[1:]:
            value = value + ref[u].astype(F32)
        return value

    return total


def enter_kernel(plan, place, *refs):
    refs = list(refs)
    own, sums = refs.pop(0), chip_order(take(refs, plan.chips))
    solved, message = refs

    def write(made):
        for _, u, value in made:
            solved[u] = value
            message[u] = value.astype(BF16)

    coupled = add_up([own] + sums[1:])
    level_forward(plan, place, 1, sums, [None] * plan.n_col, coupled, write)


def decode(plan, place, core, pieces):
    def reader(row, col):
        return lambda tile: (row[0, tile], col[0, tile + 64])

    readers = []
    for chip, piece in enumerate(pieces):
        raw = piece[plan.tile_rows : plan.inverse_at, :].astype(F32).astype(jnp.int32)[0:1]
        owner = raw // plan.rows_dev * plan.n_col + (place[1] ^ (2 * chip + core))
        readers.append(reader(raw, owner * plan.rows_dev + raw % plan.rows_dev))
    return readers


def multiply_forward(plan, place, core, pieces, left, right, totals):
    half, width = plan.block, plan.slice
    for piece, at in zip(pieces, decode(plan, place, core, pieces)):
        for k in range(plan.tiles // 4):
            matrix = piece[2 * k * half : (2 * k + 2) * half, :]
            tiles = [at(4 * k + n) for n in range(4)]
            vectors = [(right if n % 2 else left)[col] for n, (row, col) in enumerate(tiles)]
            product = lax.dot_general(jnp.concatenate(vectors, axis=0), matrix, NT, preferred_element_type=F32)
            for n, total in enumerate(totals):
                total[tiles[n][0]] += product[n * width : (n + 1) * width]


def multiply_backward(plan, place, core, pieces, upper_left, upper_right, left, right):
    half, width = plan.block, plan.slice
    for piece, at in zip(pieces, decode(plan, place, core, pieces)):
        for k in range(plan.tiles // 4):
            matrix = piece[2 * k * half : (2 * k + 2) * half, :]
            tiles = [at(4 * k + n) for n in range(4)]
            vectors = [(upper_right if n > 1 else upper_left)[row] for n, (row, col) in enumerate(tiles)]
            product = jnp.dot(jnp.concatenate(vectors, axis=0), matrix, preferred_element_type=F32)
            for n, (row, col) in enumerate(tiles):
                (right if n % 2 else left)[col] += product[n * width : (n + 1) * width]


def put_shares(plan, place, left, right, out):
    for m in range(plan.n_row):
        for u in range(plan.n_col):
            at = (place[0] ^ m) * plan.n_col + u
            out[m][u] = join_halves(left, right, at, plan.block).astype(out[m].dtype)


def clear(refs):
    for ref in refs:
        ref[...] = jnp.zeros_like(ref)


def forward_near_kernel(coupling, plan, place, *refs):
    refs = list(refs)
    pieces, received = views(plan, coupling, take(refs, 1)), take(refs, plan.n_row)
    left, right = take(refs, 2)
    totals = refs
    for m in range(plan.n_row):
        for u in range(plan.n_col):
            at = (place[0] ^ m) * plan.n_col + u
            store_halves(left, right, at, received[m][u].astype(F32), plan.block)
    clear(totals)
    multiply_forward(plan, place, 0, pieces, left, right, totals)


def forward_far_kernel(coupling, plan, place, *refs):
    refs = list(refs)
    last = coupling == plan.levels - 1
    sums, stacks = chip_order(take(refs, plan.chips)), take(refs, 2)
    left, right = take(refs, 2)
    near_totals, keep = take(refs, 4), refs.pop(0)
    out = take(refs, plan.n_row if last else 1)
    totals = take(refs, 4)
    pieces = views(plan, coupling, stacks)
    near, far = pieces[: plan.chips], pieces[plan.chips :]
    clear(totals)
    multiply_forward(plan, place, 1, far, left, right, totals)

    if last:
        upper_left, upper_right, back_left, back_right = refs

    def add(refs, at):
        return sum((ref[at] for ref in refs[1:]), refs[0][at])

    def coupled(u):
        all_totals = near_totals + totals
        low, high = all_totals[0:2] + all_totals[4:6], all_totals[2:4] + all_totals[6:8]
        first = add(low, 2 * u) + pltpu.roll(add(high, 2 * u), plan.block, 1)
        second = add(high, 2 * u + 1) + pltpu.roll(add(low, 2 * u + 1), plan.block, 1)
        return jnp.where(low_lanes(first.shape, plan.block), first, second)

    def write(made):
        for _, u, value in made:
            keep[u] = value
            out[0][u] = value.astype(BF16)

    def write_top(made):
        made = [(u, apply_pair_transposed(inverse, value, plan.block)) for inverse, u, value in made]
        for u, value in made:
            keep[u] = value.astype(BF16)
            store_halves(upper_left, upper_right, u, value, plan.block)

    level_forward(plan, place, coupling + 1, sums, pieces, coupled, write_top if last else write)
    if last:
        clear([back_left, back_right])
        multiply_backward(plan, place, 0, near, upper_left, upper_right, back_left, back_right)
        multiply_backward(plan, place, 1, far, upper_left, upper_right, back_left, back_right)
        put_shares(plan, place, back_left, back_right, out)


def backward_kernel(level, plan, place, *refs):
    refs = list(refs)
    sums, pieces = chip_order(take(refs, plan.chips)), views(plan, level - 1, take(refs, 2))
    shares = take(refs, plan.n_row)
    solved, keep = take(refs, 2)
    out = take(refs, plan.n_row)
    upper_left, upper_right, left, right = refs
    clear([left, right])
    back = add_up(shares)

    def write(u, value):
        keep[u] = value.astype(BF16)
        store_halves(upper_left, upper_right, u, value, plan.block)

    level_backward(plan, place, level, sums, pieces, lambda u: solved[u] - back(u), write)
    for core in range(2):
        here = pieces[core * plan.chips : (core + 1) * plan.chips]
        multiply_backward(plan, place, core, here, upper_left, upper_right, left, right)
    put_shares(plan, place, left, right, out)


def leave_kernel(plan, place, *refs):
    refs = list(refs)
    sums, shares = chip_order(take(refs, plan.chips)), take(refs, plan.n_row)
    solved = refs.pop(0)
    above, out = take(refs, plan.levels - 1), refs
    back = add_up(shares)

    def write(u, value):
        for message in out:
            message[u] = value.astype(BF16)

    level_backward(plan, place, 1, sums, [None] * plan.n_col, lambda u: solved[u] - back(u), write)
    for chip, message in enumerate(out):
        base = (place[1] ^ (2 * chip)) // 2 * 2
        for core in range(2):
            for n, level in enumerate(above):
                message[plan.n_col + core * (plan.levels - 1) + n] = level[base + core]


def on_device(n_row, n_col, factor_tiles, tile_row, tile_col, right_sides, diag_inverse):
    plan = Plan(n_row, n_col, factor_tiles, right_sides)
    levels, chips = plan.levels, plan.chips

    def array(shape, kind=BF16):
        return jax.ShapeDtypeStruct(shape, kind)

    def over_row(value, m):
        return lax.ppermute(value, "row", [(i, i ^ m) for i in range(n_row)])

    def over_col(value, m):
        return lax.ppermute(value, "col", [(i, i ^ m) for i in range(n_col)])

    def gather_row(value):
        return [value] + [over_row(value, m) for m in range(1, n_row)]

    def exchange_row(values):
        return [values[0]] + [over_row(values[m], m) for m in range(n_row - 1, 0, -1)]

    def exchange_chips(values):
        return [values[0]] + [over_col(values[m], 2 * m) for m in range(1, chips)]

    def after(values, *others):
        return lax.optimization_barrier((values, others))[0]

    column = (plan.padded, plan.lanes)
    slices = (n_col, plan.slice, plan.lanes)
    dma = pltpu.SemaphoreType.DMA
    x0 = lax.dot_general(right_sides[0], diag_inverse[0], (((1,), (0,)), ((), ())), precision=lax.Precision.HIGHEST)
    owner = jnp.arange(plan.lanes) // plan.block
    x0 = sum(jnp.where(owner == b, x0[b], 0.0) for b in range(plan.rows_dev))
    x0 = x0.reshape(n_col, plan.real, plan.lanes)
    x0 = jnp.pad(x0, ((0, 0), (0, plan.slice - plan.real), (0, 0))).reshape(column)
    message = x0.astype(BF16)
    tile_row, tile_col = tile_row.transpose(0, 2, 1), tile_col.transpose(0, 2, 1)
    message, tile_row, tile_col = lax.optimization_barrier((message, tile_row, tile_col))
    received = gather_row(message)
    dense, side_slices, inverse_one, *held = call(
        plan, pack_kernel,
        [array((n_row, plan.own * plan.block, plan.lanes)), array((levels,) + column),
         array((plan.block // plan.slice, plan.slice, plan.lanes))]
        + [array((1, plan.payload_rows(), plan.lanes))] * (levels - 1),
        (tile_row, tile_col, factor_tiles, right_sides, diag_inverse),
        scalars=2,
    )

    def join(held, other):
        shape = (2 * held.shape[0],) + held.shape[1:]
        return call(plan, join_kernel, [array(shape)], [held, other])[0]

    def step(held, coupling):
        bit = held.shape[0] if coupling % 2 else chips // 2 // held.shape[0]
        return held, over_col(held, 2 * bit)

    held = [step(value, s) for s, value in enumerate(after(held, received), 1)]
    keep, keep_extra, send = call(
        plan, near_forward_kernel,
        [array((chips,) + slices, F32), array((chips, plan.extra()) + slices[1:]),
         array((chips, n_col + plan.extra()) + slices[1:])],
        [dense] + received + [side_slices, inverse_one],
        [pltpu.VMEM((n_col,) + column, F32)],
    )
    swapped = over_col(send, 1)
    made = call(
        plan, add_kernel, [array(slices, F32)] + [array((n_col + 2 * plan.extra(),) + slices[1:])] * chips,
        [keep, keep_extra, swapped],
    )
    own, sums = made[0], exchange_chips(made[1:])
    held = [join(*held[0])] + [join(*value) for value in after(held[1:], sums)]
    if chips > 2:
        held = [step(value, s) for s, value in enumerate(held, 1)]
    solved, message = call(
        plan, enter_kernel, [array(slices, F32), array(slices)], [own] + chip_order(sums)
    )
    solved = [None, solved]

    halves = array((plan.blocks, plan.slice, plan.lanes))
    total = array((plan.own, plan.slice, plan.lanes), F32)
    totals = [pltpu.VMEM(total.shape, F32)] * 4
    backward = [pltpu.VMEM(total.shape, BF16)] * 2 + [pltpu.VMEM(halves.shape, F32)] * 2
    partial = [array(slices, F32)] + [array(slices)] * (n_row - 1)
    pieces = [None]
    for s in range(1, levels):
        received = gather_row(message)
        if s == 1 and chips > 2:
            received, held = lax.optimization_barrier((received, held))
            held = [join(*value) for value in held]
            while held[0].shape[0] < chips:
                held = [join(*step(value, n)) for n, value in enumerate(held, 1)]
        pieces.append([held[s - 1], over_col(held[s - 1], 1)])
        near = call(
            plan, functools.partial(forward_near_kernel, s), [halves] * 2 + [total] * 4,
            pieces[s][:1] + received,
        )
        last = s == levels - 1
        made = call(
            plan, functools.partial(forward_far_kernel, s),
            [array(slices, BF16 if last else F32)] + (partial if last else [array(slices)]),
            chip_order(sums) + pieces[s] + list(near),
            totals + (backward if last else []),
        )
        if not last:
            solved.append(made[0])
            message = made[1]
    results = [made[0]]
    shares = exchange_row(made[1:])
    for level in range(levels - 1, 1, -1):
        made = call(
            plan, functools.partial(backward_kernel, level), [array(slices)] + partial,
            chip_order(sums) + pieces[level - 1] + shares + [solved[level]],
            backward,
        )
        results.insert(0, made[0])
        shares = exchange_row(made[1:])
    messages = call(
        plan, leave_kernel, [array((n_col + 2 * (levels - 1),) + slices[1:])] * chips,
        chip_order(sums) + shares + [solved[1]] + results,
    )
    messages = exchange_chips(messages)
    messages = chip_order(messages) + chip_order([over_col(value, 1) for value in messages])
    shares = call(
        plan, near_backward_kernel, [array(column, F32)] + [array(column)] * (n_row - 1), [dense] + messages,
        [pltpu.VMEM((plan.padded, n_col * plan.lanes), BF16)],
    )
    shares = exchange_row(shares)
    result = array(right_sides.shape, F32)
    upper = call(
        plan, upper_out_kernel, [result], messages,
        [pltpu.VMEM((levels,) + column, BF16), pltpu.VMEM((levels,) + right_sides.shape[1:], F32), dma(())],
        raw_out=True,
    )[0]
    args = [diag_inverse, x0] + shares + [upper]
    return call(
        plan, last_kernel, [result], args, [pltpu.VMEM(right_sides.shape[1:], F32), dma(())],
        raw=(len(args) - 1,), raw_out=True, aliases={len(args) - 1: 0},
    )[0]


def solution(mesh):
    return jax.shard_map(
        functools.partial(on_device, mesh.shape["row"], mesh.shape["col"]),
        mesh=mesh,
        in_specs=(
            P(None, "row", None, "col"),
            P(None, "row", "col"),
            P(None, "row", "col"),
            P(None, ("col", "row"), None, None),
            P(None, None, ("col", "row")),
        ),
        out_specs=P(None, ("col", "row"), None, None),
        check_vma=False,
    )
```
